1024 devices in a mesh: row: 64 (over x, z), col: 16 (over y, core).
Axes of the slice: x: 4, y: 8, z: 16, core: 2. Of those that a mesh axis runs over, the one named last changes fastest.
Arguments:
- start: float32 [131072, 64], P(('row', 'col')), may hold values from -6 to 6
- degrees: int32 [131072], P(('row', 'col')), may hold values from 16 to 64
- blocks: float32 [64, 16, 32, 128, 128], P('row', 'col'), may hold values from -0.09375 to 0.09375
- block_rows: int32 [64, 16, 32], P('row', 'col'), may hold values from 0 to 15
- block_cols: int32 [64, 16, 32], P('row', 'col'), may hold values from 0 to 63
- block_counts: int32 [64, 16], P('row', 'col'), may hold values from 1 to 32, as said below
Outputs:
- basis: float32 [131072, 64], P(('row', 'col'))
- ritz: float32 [64, 64], replicated
The draws below stay inside these ranges and needn't reach their ends.
Inputs may be any that keep to these rules, and one draw needn't show every extreme that they name: `block_counts`: live slots of a tile; every draw has a tile with all 32 slots live, at a drawn place.
All inputs are finite; a program needn't handle non-finite values.
Results may differ from the reference program's by a relative error of at most 0.0003.
Values sent between devices are 32-bit elements; how exact they have to be, the bound alone decides.
No kernel may reach another device: no remote copies, remote signals or barrier semaphores. Data moves between devices by JAX's collectives and lax.ppermute only.
A program may use at most 32 MiB of HBM per device.

```python
import jax
import jax.numpy as jnp
from jax import lax

F = 64
BS = 128
V_DEV = 128
NB = 32
PASSES = 1
NODES = 131072
RB = 16
CB = 64
N_ROW = 64
N_COL = 16


def draw_block_counts(key, part):
    key = jax.random.fold_in(key, 11)
    key_shift, key_full = jax.random.split(key)
    shifts = jax.random.randint(key_shift, (N_ROW, N_COL), 0, 4)
    counts = jnp.maximum(NB // jnp.left_shift(jnp.int32(1), shifts), 1).astype(jnp.int32)
    chosen = jax.random.randint(key_full, (), 0, N_ROW * N_COL)
    flat = counts.reshape(-1).at[chosen].set(NB)
    return flat.reshape(N_ROW, N_COL).astype(jnp.int32)


def touch_ends(result, stream_key, least, top_value):
    extent = result.shape
    spot = [jax.random.randint(jax.random.fold_in(stream_key, axis), (), 0, extent[axis]) for axis in range(len(extent))]
    result = result.at[tuple(spot)].set(least)
    longest = extent.index(max(extent))
    spot[longest] = (spot[longest] + 1) % extent[longest]
    return result.at[tuple(spot)].set(top_value)


def block_levels(key, extent, cuts, least, largest):
    gain, own = 1.0, jax.random.fold_in(key, 6)
    for axis_at, parts in cuts:
        draws = jnp.exp(jax.random.uniform(jax.random.fold_in(own, axis_at), (parts,), jnp.float32, least / len(cuts), largest / len(cuts)))
        gain = gain * jnp.repeat(draws, extent[axis_at] // parts).reshape([-1 if axis == axis_at else 1 for axis in range(len(extent))])
    return gain


def gaussian(stream_key, extent, deviation, bound, cuts=(), held_as=jnp.bfloat16):
    loudness = block_levels(stream_key, extent, cuts, -0.22, 0.18) if cuts else 1.0
    drawn = jax.random.normal(stream_key, extent, jnp.float32) * deviation * loudness
    return jnp.minimum(jnp.maximum(drawn, -bound), bound).astype(held_as)


def setup_inputs(seed: int = 0) -> dict:
    key_of = jax.random.split(jax.random.key(seed), 7)
    start = gaussian(key_of[0], (NODES, F), 1.0, 6.0, ((0, 1024),), jnp.float32)
    degrees = touch_ends(jax.random.randint(key_of[1], (NODES,), 16, 65), jax.random.fold_in(key_of[1], 1), 16, 64).astype(jnp.int32)
    blocks = gaussian(key_of[2], (N_ROW, N_COL, NB, BS, BS), (BS * NB) ** -0.5, 0.09375, ((0, 64), (1, 16)), jnp.float32)
    block_rows = touch_ends(jax.random.randint(key_of[3], (N_ROW, N_COL, NB), 0, RB), jax.random.fold_in(key_of[3], 1), 0, RB - 1).astype(jnp.int32)
    block_cols = touch_ends(jax.random.randint(key_of[4], (N_ROW, N_COL, NB), 0, CB), jax.random.fold_in(key_of[4], 1), 0, CB - 1).astype(jnp.int32)
    block_counts = draw_block_counts(jax.random.fold_in(key_of[6], 71), 0)
    return dict(start=start, degrees=degrees, blocks=blocks, block_rows=block_rows, block_cols=block_cols, block_counts=block_counts)


def apply_op(vectors, scale, blocks, block_rows, block_cols, block_counts):
    scaled = vectors * scale[:, None]
    pieces = scaled.reshape(N_ROW, N_COL, V_DEV, F)
    column_blocks = jnp.transpose(pieces, (1, 0, 2, 3)).reshape(N_COL, CB, BS, F)
    col_index = jnp.arange(N_COL, dtype=jnp.int32)[:, None]

    def one_row(items):
        tile_blocks, tile_rows, tile_cols, tile_counts = items
        gathered = column_blocks[col_index, tile_cols]
        live = (jnp.arange(NB, dtype=jnp.int32)[None, :] < tile_counts[:, None]).astype(jnp.float32)
        prod = jnp.einsum('cbik,cbkf->cbif', tile_blocks, gathered, precision=lax.Precision.HIGHEST)
        prod = prod * live[:, :, None, None]
        onehot = (tile_rows[:, :, None] == jnp.arange(RB, dtype=jnp.int32)[None, None, :]).astype(jnp.float32)
        summed = jnp.einsum('cbt,cbif->tif', onehot, prod, precision=lax.Precision.HIGHEST)
        return summed.reshape(RB * BS, F)
    rows_out = lax.map(one_row, (blocks, block_rows, block_cols, block_counts))
    return rows_out.reshape(NODES, F) * scale[:, None]

def orthonormal(filtered):
    gram_matrix = jnp.dot(filtered.T, filtered, precision=lax.Precision.HIGHEST) / NODES
    lower = jnp.linalg.cholesky(gram_matrix)
    return jax.scipy.linalg.solve_triangular(lower, filtered.T, lower=True).T

def reference(start, degrees, blocks, block_rows, block_cols, block_counts):
    scale = jnp.sqrt(16.0 / degrees.astype(jnp.float32))

    def operator(vectors):
        return apply_op(vectors, scale, blocks, block_rows, block_cols, block_counts)
    current = orthonormal(start)
    filtered = current
    for step in range(PASSES):
        first = operator(current)
        filtered = 2.0 * operator(first) - current
        if step + 1 < PASSES:
            current = orthonormal(filtered)
    basis = orthonormal(filtered)
    ritz = jnp.dot(basis.T, operator(basis), precision=lax.Precision.HIGHEST) / NODES
    return (basis, ritz)
```

```python
import functools

import jax
import jax.numpy as jnp
from jax import lax
from jax.experimental import pallas as pl
from jax.experimental.pallas import tpu as pltpu
from jax.sharding import Mesh, PartitionSpec as P

HIGHEST = lax.Precision.HIGHEST
AXES = ("x", "z", "y", "core")
CONTRACT_LAST = (((1,), (1,)), ((), ()))


def exchange(chunks, axes):
    return lax.all_to_all(chunks, axes, 0, 0, tiled=True)


def to_all(value, axes):
    copies = lax.axis_size(axes)
    return exchange(jnp.broadcast_to(value[None], (copies, *value.shape)), axes)


def tile_kernel(rows_ref, cols_ref, count_ref, blocks_ref, gathered_ref, out_ref):
    out_ref[...] = jnp.zeros_like(out_ref)
    count = count_ref[0]
    for slot in range(blocks_ref.shape[0]):
        live = (slot < count).astype(jnp.float32)
        product = lax.dot_general(
            gathered_ref[cols_ref[slot]],
            blocks_ref[slot],
            CONTRACT_LAST,
            precision=HIGHEST,
            preferred_element_type=jnp.float32,
        )
        out_ref[rows_ref[slot]] += product * live


def tile_product(gathered, blocks, rows, cols, count, row_blocks):
    smem = pl.BlockSpec(memory_space=pltpu.SMEM)
    vmem = pl.BlockSpec(memory_space=pltpu.VMEM)
    width, nodes = gathered.shape[1:]
    return pl.pallas_call(
        tile_kernel,
        out_shape=jax.ShapeDtypeStruct((row_blocks, width, nodes), jnp.float32),
        in_specs=[smem, smem, smem, vmem, vmem],
        out_specs=vmem,
        compiler_params=pltpu.CompilerParams(vmem_limit_bytes=24 * 2**20),
    )(rows, cols, count, blocks, gathered)


def gram(left, right):
    return lax.dot_general(left, right, CONTRACT_LAST, precision=HIGHEST)


def matmul(left, right):
    return jnp.dot(left, right, precision=HIGHEST)


def inverse_factor(gram_matrix):
    lower = jnp.linalg.cholesky(gram_matrix)
    eye = jnp.eye(gram_matrix.shape[0], dtype=gram_matrix.dtype)
    return jax.scipy.linalg.solve_triangular(lower, eye, lower=True)


def fold(square):
    half = square.shape[0] // 2
    return jnp.concatenate([square[:half], square[half:]], axis=1)


def unfold(folded):
    half = folded.shape[1] // 2
    return jnp.concatenate([folded[:, :half], folded[:, half:]], axis=0)


def shards(start, degrees, blocks, block_rows, block_cols, block_counts):
    row_devices = lax.axis_size(("x", "z"))
    col_devices = lax.axis_size(("y", "core"))
    nodes, width = start.shape
    nodes_all = nodes * row_devices * col_devices
    scale = jnp.sqrt(16.0 / degrees.astype(jnp.float32))[None, :]
    tile_blocks = blocks.reshape(blocks.shape[2:])
    rows = block_rows.reshape(-1)
    y_devices = lax.axis_size("y")
    rows = (rows % 2) * y_devices + rows // 2
    cols = block_cols.reshape(-1)
    count = block_counts.reshape(-1)

    def gather_rows(vectors, extra=None):
        scaled = vectors * scale
        if extra is not None:
            scaled = jnp.concatenate([scaled, fold(extra)], axis=0)
        along_z = lax.all_gather(scaled, "z", axis=0, tiled=False)
        pieces = along_z[:, :width]
        if extra is None:
            everywhere = to_all(pieces, "x")
            return everywhere.reshape(row_devices, width, nodes), None
        summed = along_z[:, width:].sum(0)
        packed = jnp.concatenate([pieces.reshape(-1, nodes), summed], axis=0)
        everywhere = to_all(packed, "x").reshape(lax.axis_size("x"), -1, nodes)
        cut = pieces.shape[0] * width
        return everywhere[:, :cut].reshape(row_devices, width, nodes), everywhere[:, cut:].sum(0)

    def product(gathered):
        return tile_product(gathered, tile_blocks, rows, cols, count, col_devices)

    def reduce_cols(partial, extra=None):
        halves = partial.reshape(2, -1, nodes)
        if extra is not None:
            halves = jnp.concatenate([halves, jnp.broadcast_to(extra[None], (2, *extra.shape))], axis=1)
        halves = exchange(halves, "core").sum(0)
        cut = y_devices * width
        chunks = halves[:cut].reshape(y_devices, width, nodes)
        if extra is not None:
            rest = jnp.broadcast_to(halves[cut:][None], (y_devices, *extra.shape))
            chunks = jnp.concatenate([chunks, rest], axis=1)
        done = exchange(chunks, "y").sum(0)
        if extra is None:
            return done * scale, None
        return done[:width] * scale, unfold(done[width:])

    first = start.T
    gathered, row_sum = gather_rows(first, gram(first, first))
    once, gram_first = reduce_cols(product(gathered), row_sum)
    gathered, _ = gather_rows(once)
    twice, _ = reduce_cols(product(gathered))
    filtered = matmul(inverse_factor(gram_first / nodes_all), 2.0 * twice - first)

    gathered, _ = gather_rows(filtered)
    own_rows = lax.all_gather(filtered * scale, ("y", "core"), axis=0, tiled=False)
    own_rows = own_rows.reshape(y_devices, 2, width, nodes).swapaxes(0, 1).reshape(col_devices, width, nodes)
    partial = product(gathered)
    projected = jnp.einsum("rfi,rgi->fg", own_rows, partial, precision=HIGHEST)
    both = jnp.concatenate([gram(filtered, filtered), projected], axis=1)
    both = exchange(both.reshape(col_devices, -1, 2 * width), ("y", "core")).sum(0)
    both = to_all(both, ("x", "z")).reshape(row_devices, -1, 2 * width).sum(0)
    both = to_all(both, ("y", "core")).reshape(width, 2 * width) / nodes_all
    inverse = inverse_factor(both[:, :width])
    basis = matmul(inverse, filtered)
    ritz = matmul(matmul(inverse, both[:, width:]), inverse.T)
    return (basis.T, ritz)


def solution(mesh):
    sizes = (4, 16, 8, 2)
    return jax.shard_map(
        shards,
        mesh=Mesh(mesh.devices.reshape(sizes), AXES),
        in_specs=(
            P(AXES, None),
            P(AXES),
            P(("x", "z"), ("y", "core"), None, None, None),
            P(("x", "z"), ("y", "core"), None),
            P(("x", "z"), ("y", "core"), None),
            P(("x", "z"), ("y", "core")),
        ),
        out_specs=(P(AXES, None), P()),
        check_vma=False,
    )
```

```python
import functools

import jax
import jax.numpy as jnp
from jax import lax
from jax.experimental import pallas as pl
from jax.experimental.pallas import tpu as pltpu
from jax.sharding import Mesh, PartitionSpec as P

HIGHEST = lax.Precision.HIGHEST
AXES = ("x", "z", "y", "core")
CONTRACT_LAST = (((1,), (1,)), ((), ()))


def exchange(chunks, axes):
    return lax.all_to_all(chunks, axes, 0, 0, tiled=True)


def to_all(value, axes):
    copies = lax.axis_size(axes)
    return exchange(jnp.broadcast_to(value[None], (copies, *value.shape)), axes)


def split(value):
    high = value.astype(jnp.bfloat16)
    return high, (value - high.astype(jnp.float32)).astype(jnp.bfloat16)


def dot_pieces(left, right):
    return lax.dot_general(left, right, CONTRACT_LAST, preferred_element_type=jnp.float32)


def add_slots(rows_ref, cols_ref, count_ref, blocks_ref, gathered_ref, sums_ref):
    sums_ref[...] = jnp.zeros_like(sums_ref)
    count = count_ref[0]
    width = sums_ref.shape[1]
    for slot in range(blocks_ref.shape[0]):
        live = (slot < count).astype(jnp.float32)
        high, low = split(gathered_ref[cols_ref[slot]] * live)
        block_high, block_low = split(blocks_ref[slot])
        both = dot_pieces(jnp.concatenate([high, low], axis=0), block_high)
        sums_ref[rows_ref[slot]] += both[:width] + both[width:] + dot_pieces(high, block_low)


def tile_kernel(rows_ref, cols_ref, count_ref, blocks_ref, gathered_ref, out_ref):
    add_slots(rows_ref, cols_ref, count_ref, blocks_ref, gathered_ref, out_ref)


def tile_rider_kernel(rows_ref, cols_ref, count_ref, blocks_ref, gathered_ref, rider_ref, out_ref, rider_out_ref):
    add_slots(rows_ref, cols_ref, count_ref, blocks_ref, gathered_ref, out_ref)
    rider_out_ref[...] = jnp.sum(rider_ref[...], axis=0)


def project_kernel(rows_ref, cols_ref, count_ref, blocks_ref, gathered_ref, own_ref, out_ref, rider_out_ref, sums_ref):
    add_slots(rows_ref, cols_ref, count_ref, blocks_ref, gathered_ref, sums_ref)
    row_blocks, width, _ = sums_ref.shape
    half = row_blocks // 2
    total = jnp.zeros((width, width), jnp.float32)
    rider = jnp.zeros(rider_out_ref.shape, jnp.float32)
    for piece in range(row_blocks):
        total += lax.dot_general(
            own_ref[piece, :width],
            sums_ref[(piece % 2) * half + piece // 2],
            CONTRACT_LAST,
            precision=HIGHEST,
            preferred_element_type=jnp.float32,
        )
        rider += own_ref[piece, width:]
    out_ref[...] = fold(total)
    rider_out_ref[...] = rider


def sum_kernel(chunks_ref, rider_ref, copies_ref, rider_out_ref):
    copies_ref[...] = jnp.broadcast_to(jnp.sum(chunks_ref[...], axis=0)[None], copies_ref.shape)
    rider_out_ref[...] = jnp.sum(rider_ref[...], axis=0, keepdims=True)


def inverse_kernel(nodes_all, folded_ref, out_ref):
    size = out_ref.shape[0]
    shape = (size, 2 * size)
    gram_matrix = unfold(jnp.sum(folded_ref[...], axis=0)) / nodes_all
    row_of = lax.broadcasted_iota(jnp.int32, shape, 0)
    eye = (lax.broadcasted_iota(jnp.int32, (size, size), 0) == lax.broadcasted_iota(jnp.int32, (size, size), 1)).astype(
        jnp.float32
    )
    work = jnp.concatenate([gram_matrix, eye], axis=1)
    for j in range(0, size, 2):
        left = jnp.broadcast_to(work[:, j : j + 1], shape)
        right = jnp.broadcast_to(work[:, j + 1 : j + 2], shape)
        upper, lower = work[j : j + 1], work[j + 1 : j + 2]
        inverse_pivot = 1.0 / left[j : j + 1]
        ratio = left[j + 1 : j + 2] * inverse_pivot
        next_pivot = right[j + 1 : j + 2] - ratio * left[j + 1 : j + 2]
        lower = (lower - ratio * upper) * (1.0 / next_pivot)
        right = jnp.where(row_of > j + 1, right - left * ratio, 0.0)
        left = jnp.where(row_of > j, left, 0.0)
        work = work - left * (upper * inverse_pivot) - right * lower
    diagonal = jnp.sum(work[:, :size] * eye, axis=1, keepdims=True)
    out_ref[...] = work[:, size:] * lax.rsqrt(diagonal)


def ritz_kernel(nodes_all, inverse_ref, folded_ref, out_ref):
    inverse = inverse_ref[...]
    half = jnp.dot(inverse, unfold(folded_ref[...]) / nodes_all, precision=HIGHEST, preferred_element_type=jnp.float32)
    out_ref[...] = lax.dot_general(
        half, inverse, CONTRACT_LAST, precision=HIGHEST, preferred_element_type=jnp.float32
    )


SMEM = pl.BlockSpec(memory_space=pltpu.SMEM)
VMEM = pl.BlockSpec(memory_space=pltpu.VMEM)


def call_kernel(kernel, ins, outs, scratch=(), flops=0):
    return pl.pallas_call(
        kernel,
        out_shape=[jax.ShapeDtypeStruct(shape, jnp.float32) for shape in outs],
        in_specs=[SMEM if value.dtype == jnp.int32 else VMEM for value in ins],
        out_specs=[VMEM] * len(outs),
        scratch_shapes=list(scratch),
        compiler_params=pltpu.CompilerParams(vmem_limit_bytes=24 * 2**20),
        cost_estimate=pl.CostEstimate(flops=flops, bytes_accessed=4 * sum(x.size for x in ins), transcendentals=0),
    )(*ins)


def gram(left, right):
    return lax.dot_general(left, right, CONTRACT_LAST, precision=HIGHEST)


def matmul(left, right):
    return jnp.dot(left, right, precision=HIGHEST)


def fold(square):
    half = square.shape[0] // 2
    return jnp.concatenate([square[:half], square[half:]], axis=1)


def unfold(folded):
    half = folded.shape[1] // 2
    return jnp.concatenate([folded[:, :half], folded[:, half:]], axis=0)


def shards(start, degrees, blocks, block_rows, block_cols, block_counts):
    row_devices = lax.axis_size(("x", "z"))
    col_devices = lax.axis_size(("y", "core"))
    nodes, width = start.shape
    nodes_all = nodes * row_devices * col_devices
    scale = jnp.sqrt(16.0 / degrees.astype(jnp.float32))[None, :]
    tile_blocks = blocks.reshape(blocks.shape[2:])
    rows = block_rows.reshape(-1)
    y_devices = lax.axis_size("y")
    rows = (rows % 2) * y_devices + rows // 2
    cols = block_cols.reshape(-1)
    count = block_counts.reshape(-1)

    tile = (rows, cols, count, tile_blocks)
    sums_shape = (col_devices, width, nodes)
    folded_shape = (width // 2, nodes)
    copies_shape = (lax.axis_size("x"), lax.axis_size("z"), width, nodes)
    serial = 5 * 10**9

    def gather(value, axes):
        return lax.all_gather(value, axes, axis=0, tiled=False)

    def spread(along_z):
        return jnp.broadcast_to(along_z[None, :, :width], copies_shape), along_z[:, width:].sum(0)

    def gather_x(copies):
        return exchange(copies, "x").reshape(row_devices, width, nodes)

    def reduce_cols(partial):
        halves = exchange(partial.reshape(2, -1, nodes), "core").sum(0)
        return exchange(halves.reshape(y_devices, width, nodes), "y").sum(0) * scale

    def inverse_factor(folded):
        (inverse,) = call_kernel(
            functools.partial(inverse_kernel, nodes_all), (folded,), [(width, width)], flops=serial
        )
        return inverse

    first = start.T
    copies, rider = spread(gather(jnp.concatenate([first * scale, fold(gram(first, first))], axis=0), "z"))
    partial, rider = call_kernel(
        tile_rider_kernel, (*tile, gather_x(copies), gather(rider, ("y", "core"))), [sums_shape, folded_shape]
    )
    once = reduce_cols(partial)

    copies, _ = spread(gather(once * scale, "z"))
    inverse = inverse_factor(gather(rider, "x"))
    (partial,) = call_kernel(tile_kernel, (*tile, gather_x(copies)), [sums_shape])
    filtered = matmul(inverse, 2.0 * reduce_cols(partial) - first)

    scaled = filtered * scale
    copies, rider = spread(gather(jnp.concatenate([scaled, fold(gram(filtered, filtered))], axis=0), "z"))
    own_rows = gather(jnp.concatenate([scaled, rider], axis=0), ("y", "core"))
    projected, rider = call_kernel(
        project_kernel,
        (*tile, gather_x(copies), own_rows),
        [folded_shape, folded_shape],
        [pltpu.VMEM(sums_shape, jnp.float32)],
    )
    chunk_shape = (folded_shape[0] // col_devices, nodes)
    chunks = exchange(projected.reshape(col_devices, *chunk_shape), ("y", "core"))
    copies, rider = call_kernel(
        sum_kernel, (chunks, gather(rider, "x")), [(row_devices, *chunk_shape), (1, *folded_shape)]
    )
    inverse = inverse_factor(rider)
    basis = matmul(inverse, filtered)
    projected = exchange(copies, ("x", "z")).sum(0)
    projected = to_all(projected, ("y", "core")).reshape(folded_shape)
    (ritz,) = call_kernel(functools.partial(ritz_kernel, nodes_all), (inverse, projected), [(width, width)])
    return (basis.T, ritz)


def solution(mesh):
    sizes = (4, 16, 8, 2)
    return jax.shard_map(
        shards,
        mesh=Mesh(mesh.devices.reshape(sizes), AXES),
        in_specs=(
            P(AXES, None),
            P(AXES),
            P(("x", "z"), ("y", "core"), None, None, None),
            P(("x", "z"), ("y", "core"), None),
            P(("x", "z"), ("y", "core"), None),
            P(("x", "z"), ("y", "core")),
        ),
        out_specs=(P(AXES, None), P()),
        check_vma=False,
    )
```

```python
import functools

import jax
import jax.numpy as jnp
from jax import lax
from jax.experimental import pallas as pl
from jax.experimental.pallas import tpu as pltpu
from jax.sharding import Mesh, PartitionSpec as P

HIGHEST = lax.Precision.HIGHEST
AXES = ("x", "zh", "zl", "y", "core")
ROW = ("x", "zh", "zl")
COL = ("y", "core")
CONTRACT_LAST = (((1,), (1,)), ((), ()))


def exchange(chunks, axes):
    return lax.all_to_all(chunks, axes, 0, 0, tiled=True)


def to_all(value, axes):
    copies = lax.axis_size(axes)
    return exchange(jnp.broadcast_to(value[None], (copies, *value.shape)), axes)


def split(value):
    high = value.astype(jnp.bfloat16)
    return high, (value - high.astype(jnp.float32)).astype(jnp.bfloat16)


def dot_pieces(left, right):
    return lax.dot_general(left, right, CONTRACT_LAST, preferred_element_type=jnp.float32)


def add_slots(rows_ref, cols_ref, count_ref, blocks_ref, gathered_ref, sums_ref):
    sums_ref[...] = jnp.zeros_like(sums_ref)
    count = count_ref[0]
    width = sums_ref.shape[1]
    for slot in range(blocks_ref.shape[0]):
        live = (slot < count).astype(jnp.float32)
        high, low = split(gathered_ref[cols_ref[slot]] * live)
        block_high, block_low = split(blocks_ref[slot])
        both = dot_pieces(jnp.concatenate([high, low], axis=0), block_high)
        sums_ref[rows_ref[slot]] += both[:width] + both[width:] + dot_pieces(high, block_low)


def tile_kernel(rows_ref, cols_ref, count_ref, blocks_ref, gathered_ref, out_ref):
    add_slots(rows_ref, cols_ref, count_ref, blocks_ref, gathered_ref, out_ref)


def tile_rider_kernel(rows_ref, cols_ref, count_ref, blocks_ref, gathered_ref, rider_ref, out_ref, rider_out_ref):
    add_slots(rows_ref, cols_ref, count_ref, blocks_ref, gathered_ref, out_ref)
    rider_out_ref[...] = jnp.sum(rider_ref[...], axis=0)


def project_kernel(
    rows_ref, cols_ref, count_ref, blocks_ref, gathered_ref, own_ref, gram_ref, out_ref, sums_ref
):
    add_slots(rows_ref, cols_ref, count_ref, blocks_ref, gathered_ref, sums_ref)
    row_blocks, width, _ = sums_ref.shape
    half = row_blocks // 2
    products = jnp.zeros((2 * width, 2 * width), jnp.float32)
    for piece in range(row_blocks):
        left = jnp.concatenate(split(own_ref[piece]), axis=0)
        right = jnp.concatenate(split(sums_ref[(piece % 2) * half + piece // 2]), axis=0)
        products += dot_pieces(left, right)
    total = products[:width, :width] + products[:width, width:] + products[width:, :width] + products[width:, width:]
    out_ref[...] = jnp.concatenate([total, gram_ref[...]], axis=1)


def sum_kernel(chunks_ref, copies_ref):
    copies_ref[...] = jnp.broadcast_to(jnp.sum(chunks_ref[...], axis=0)[None], copies_ref.shape)


def inverse_factor(gram_matrix):
    size = gram_matrix.shape[0]
    shape = (size, 2 * size)
    row_of = lax.broadcasted_iota(jnp.int32, shape, 0)
    eye = (lax.broadcasted_iota(jnp.int32, (size, size), 0) == lax.broadcasted_iota(jnp.int32, (size, size), 1)).astype(
        jnp.float32
    )
    work = jnp.concatenate([gram_matrix, eye], axis=1)
    for j in range(0, size, 2):
        left = jnp.broadcast_to(work[:, j : j + 1], shape)
        right = jnp.broadcast_to(work[:, j + 1 : j + 2], shape)
        upper, lower = work[j : j + 1], work[j + 1 : j + 2]
        inverse_pivot = 1.0 / left[j : j + 1]
        ratio = left[j + 1 : j + 2] * inverse_pivot
        next_pivot = right[j + 1 : j + 2] - ratio * left[j + 1 : j + 2]
        lower = (lower - ratio * upper) * (1.0 / next_pivot)
        right = jnp.where(row_of > j + 1, right - left * ratio, 0.0)
        left = jnp.where(row_of > j, left, 0.0)
        work = work - left * (upper * inverse_pivot) - right * lower
    diagonal = jnp.sum(work[:, :size] * eye, axis=1, keepdims=True)
    return work[:, size:] * lax.rsqrt(diagonal)


def inverse_kernel(nodes_all, folded_ref, out_ref):
    out_ref[...] = inverse_factor(unfold(folded_ref[...]) / nodes_all)


def finish_kernel(nodes_all, both_ref, filtered_ref, basis_ref, ritz_ref):
    width = filtered_ref.shape[0]
    both = both_ref[...] / nodes_all
    inverse = inverse_factor(both[:, width:])
    half = jnp.dot(inverse, both[:, :width], precision=HIGHEST, preferred_element_type=jnp.float32)
    ritz_ref[...] = lax.dot_general(
        half, inverse, CONTRACT_LAST, precision=HIGHEST, preferred_element_type=jnp.float32
    )
    basis_ref[...] = jnp.dot(inverse, filtered_ref[...], precision=HIGHEST, preferred_element_type=jnp.float32)


SMEM = pl.BlockSpec(memory_space=pltpu.SMEM)
VMEM = pl.BlockSpec(memory_space=pltpu.VMEM)


def call_kernel(kernel, ins, outs, scratch=(), flops=0):
    return pl.pallas_call(
        kernel,
        out_shape=[jax.ShapeDtypeStruct(shape, jnp.float32) for shape in outs],
        in_specs=[SMEM if value.dtype == jnp.int32 else VMEM for value in ins],
        out_specs=[VMEM] * len(outs),
        scratch_shapes=list(scratch),
        compiler_params=pltpu.CompilerParams(vmem_limit_bytes=24 * 2**20),
        cost_estimate=pl.CostEstimate(flops=flops, bytes_accessed=4 * sum(x.size for x in ins), transcendentals=0),
    )(*ins)


def gram(left, right):
    return lax.dot_general(left, right, CONTRACT_LAST, precision=HIGHEST)


def matmul(left, right):
    return jnp.dot(left, right, precision=HIGHEST)


def fold(square):
    half = square.shape[0] // 2
    return jnp.concatenate([square[:half], square[half:]], axis=1)


def unfold(folded):
    half = folded.shape[1] // 2
    return jnp.concatenate([folded[:, :half], folded[:, half:]], axis=0)


def shards(start, degrees, blocks, block_rows, block_cols, block_counts):
    row_devices = lax.axis_size(ROW)
    col_devices = lax.axis_size(COL)
    nodes, width = start.shape
    nodes_all = nodes * row_devices * col_devices
    scale = jnp.sqrt(16.0 / degrees.astype(jnp.float32))[None, :]
    tile_blocks = blocks.reshape(blocks.shape[2:])
    rows = block_rows.reshape(-1)
    y_devices = lax.axis_size("y")
    rows = (rows % 2) * y_devices + rows // 2
    zh_devices, zl_devices = lax.axis_size("zh"), lax.axis_size("zl")
    cols = block_cols.reshape(-1)
    along_z = cols % (zh_devices * zl_devices)
    cols = cols - along_z + (along_z % zl_devices) * zh_devices + along_z // zl_devices
    count = block_counts.reshape(-1)

    tile = (rows, cols, count, tile_blocks)
    sums_shape = (col_devices, width, nodes)
    serial = 5 * 10**9

    def gather(value, axes):
        return lax.all_gather(value, axes, axis=0, tiled=False)

    def gather_rows(along_zh):
        return to_all(along_zh, ("x", "zl")).reshape(row_devices, width, nodes)

    def reduce_cols(partial):
        halves = exchange(partial.reshape(2, -1, nodes), "core").sum(0)
        return exchange(halves.reshape(y_devices, width, nodes), "y").sum(0) * scale

    def sum_to(chunks, copies):
        return call_kernel(sum_kernel, (chunks,), [(copies, *chunks.shape[1:])])[0]

    first = start.T
    gathered = gather_rows(to_all(first * scale, "zh"))
    rider = gather(fold(gram(first, first)), COL)
    partial, rider = call_kernel(tile_rider_kernel, (*tile, gathered, rider), [sums_shape, rider.shape[1:]])
    once = reduce_cols(partial)

    rider = gather(rider, "x").sum(0).reshape(lax.axis_size("x"), -1, nodes)
    rider = lax.dynamic_index_in_dim(rider, lax.axis_index("x"), keepdims=False)
    along_zh = to_all(jnp.concatenate([once * scale, rider], axis=0), "zh")
    gathered = gather_rows(along_zh[:, :width])
    rider = gather(along_zh[:, width:].sum(0), ("x", "zl"))
    rider = rider.reshape(lax.axis_size("x"), zl_devices, -1, nodes).sum(1).reshape(-1, nodes)
    (inverse,) = call_kernel(
        functools.partial(inverse_kernel, nodes_all), (rider,), [(width, width)], flops=serial
    )
    (partial,) = call_kernel(tile_kernel, (*tile, gathered), [sums_shape])
    filtered = matmul(inverse, 2.0 * reduce_cols(partial) - first)

    scaled = filtered * scale
    gathered = gather_rows(to_all(scaled, "zh"))
    (projected,) = call_kernel(
        project_kernel,
        (*tile, gathered, gather(scaled, COL), gram(filtered, filtered)),
        [(width, 2 * width)],
        [pltpu.VMEM(sums_shape, jnp.float32)],
    )
    projected = exchange(projected.reshape(col_devices, -1, 2 * width), COL)
    projected = exchange(sum_to(projected, row_devices), ROW)
    projected = exchange(sum_to(projected, col_devices), COL).reshape(width, 2 * width)
    basis, ritz = call_kernel(
        functools.partial(finish_kernel, nodes_all), (projected, filtered), [(width, nodes), (width, width)]
    )
    return (basis.T, ritz)


def solution(mesh):
    sizes = (4, 8, 2, 8, 2)
    return jax.shard_map(
        shards,
        mesh=Mesh(mesh.devices.reshape(sizes), AXES),
        in_specs=(
            P(AXES, None),
            P(AXES),
            P(ROW, COL, None, None, None),
            P(ROW, COL, None),
            P(ROW, COL, None),
            P(ROW, COL),
        ),
        out_specs=(P(AXES, None), P()),
        check_vma=False,
    )
```

```python
import functools

import jax
import jax.numpy as jnp
from jax import lax
from jax.experimental import pallas as pl
from jax.experimental.pallas import tpu as pltpu
from jax.sharding import Mesh, PartitionSpec as P

HIGHEST = lax.Precision.HIGHEST
AXES = ("x", "zh", "zl", "y", "core")
ROW = ("x", "zh", "zl")
COL = ("y", "core")
CONTRACT_LAST = (((1,), (1,)), ((), ()))


def exchange(chunks, axes):
    return lax.all_to_all(chunks, axes, 0, 0, tiled=True)


def to_all(value, axes):
    copies = lax.axis_size(axes)
    return exchange(jnp.broadcast_to(value[None], (copies, *value.shape)), axes)


def split(value):
    high = value.astype(jnp.bfloat16)
    return high, (value - high.astype(jnp.float32)).astype(jnp.bfloat16)


def dot_pieces(left, right):
    return lax.dot_general(left, right, CONTRACT_LAST, preferred_element_type=jnp.float32)


def add_slots(rows_ref, cols_ref, count_ref, blocks_ref, gathered_ref, sums_ref):
    sums_ref[...] = jnp.zeros_like(sums_ref)
    count = count_ref[0]
    width = sums_ref.shape[1]
    for slot in range(blocks_ref.shape[0]):
        live = (slot < count).astype(jnp.float32)
        high, low = split(gathered_ref[cols_ref[slot]] * live)
        block_high, block_low = split(blocks_ref[slot])
        both = dot_pieces(jnp.concatenate([high, low], axis=0), block_high)
        sums_ref[rows_ref[slot]] += both[:width] + both[width:] + dot_pieces(high, block_low)


def tile_kernel(rows_ref, cols_ref, count_ref, blocks_ref, gathered_ref, out_ref):
    add_slots(rows_ref, cols_ref, count_ref, blocks_ref, gathered_ref, out_ref)


def project_kernel(
    rows_ref, cols_ref, count_ref, blocks_ref, gathered_ref, own_ref, gram_ref, out_ref, sums_ref
):
    add_slots(rows_ref, cols_ref, count_ref, blocks_ref, gathered_ref, sums_ref)
    row_blocks, width, _ = sums_ref.shape
    half = row_blocks // 2
    products = jnp.zeros((2 * width, 2 * width), jnp.float32)
    for piece in range(row_blocks):
        left = jnp.concatenate(split(own_ref[piece]), axis=0)
        right = jnp.concatenate(split(sums_ref[(piece % 2) * half + piece // 2]), axis=0)
        products += dot_pieces(left, right)
    total = products[:width, :width] + products[:width, width:] + products[width:, :width] + products[width:, width:]
    out_ref[...] = jnp.concatenate([total, gram_ref[...]], axis=1)


def sum_kernel(chunks_ref, copies_ref):
    copies_ref[...] = jnp.broadcast_to(jnp.sum(chunks_ref[...], axis=0)[None], copies_ref.shape)


def inverse_factor(gram_matrix):
    size = gram_matrix.shape[0]
    shape = (size, 2 * size)
    row_of = lax.broadcasted_iota(jnp.int32, shape, 0)
    eye = (lax.broadcasted_iota(jnp.int32, (size, size), 0) == lax.broadcasted_iota(jnp.int32, (size, size), 1)).astype(
        jnp.float32
    )
    work = jnp.concatenate([gram_matrix, eye], axis=1)
    for j in range(0, size, 2):
        left = jnp.broadcast_to(work[:, j : j + 1], shape)
        right = jnp.broadcast_to(work[:, j + 1 : j + 2], shape)
        upper, lower = work[j : j + 1], work[j + 1 : j + 2]
        inverse_pivot = 1.0 / left[j : j + 1]
        ratio = left[j + 1 : j + 2] * inverse_pivot
        next_pivot = right[j + 1 : j + 2] - ratio * left[j + 1 : j + 2]
        lower = (lower - ratio * upper) * (1.0 / next_pivot)
        right = jnp.where(row_of > j + 1, right - left * ratio, 0.0)
        left = jnp.where(row_of > j, left, 0.0)
        work = work - left * (upper * inverse_pivot) - right * lower
    diagonal = jnp.sum(work[:, :size] * eye, axis=1, keepdims=True)
    return work[:, size:] * lax.rsqrt(diagonal)


def inverse_kernel(nodes_all, folded_ref, out_ref):
    out_ref[...] = inverse_factor(unfold(jnp.sum(folded_ref[...], axis=0)) / nodes_all)


def finish_kernel(nodes_all, both_ref, filtered_ref, basis_ref, ritz_ref):
    width = filtered_ref.shape[0]
    both = both_ref[...] / nodes_all
    inverse = inverse_factor(both[:, width:])
    half = jnp.dot(inverse, both[:, :width], precision=HIGHEST, preferred_element_type=jnp.float32)
    ritz_ref[...] = lax.dot_general(
        half, inverse, CONTRACT_LAST, precision=HIGHEST, preferred_element_type=jnp.float32
    )
    basis_ref[...] = jnp.dot(inverse, filtered_ref[...], precision=HIGHEST, preferred_element_type=jnp.float32)


SMEM = pl.BlockSpec(memory_space=pltpu.SMEM)
VMEM = pl.BlockSpec(memory_space=pltpu.VMEM)


def call_kernel(kernel, ins, outs, scratch=()):
    return pl.pallas_call(
        kernel,
        out_shape=[jax.ShapeDtypeStruct(shape, jnp.float32) for shape in outs],
        in_specs=[SMEM if value.dtype == jnp.int32 else VMEM for value in ins],
        out_specs=[VMEM] * len(outs),
        scratch_shapes=list(scratch),
        compiler_params=pltpu.CompilerParams(vmem_limit_bytes=24 * 2**20),
    )(*ins)


def gram(left, right):
    return lax.dot_general(left, right, CONTRACT_LAST, precision=HIGHEST)


def matmul(left, right):
    return jnp.dot(left, right, precision=HIGHEST)


def fold(square):
    half = square.shape[0] // 2
    return jnp.concatenate([square[:half], square[half:]], axis=1)


def unfold(folded):
    half = folded.shape[1] // 2
    return jnp.concatenate([folded[:, :half], folded[:, half:]], axis=0)


def shards(start, degrees, blocks, block_rows, block_cols, block_counts):
    row_devices = lax.axis_size(ROW)
    col_devices = lax.axis_size(COL)
    nodes, width = start.shape
    nodes_all = nodes * row_devices * col_devices
    scale = jnp.sqrt(16.0 / degrees.astype(jnp.float32))[None, :]
    tile_blocks = blocks.reshape(blocks.shape[2:])
    rows = block_rows.reshape(-1)
    y_devices = lax.axis_size("y")
    rows = (rows % 2) * y_devices + rows // 2
    zh_devices, zl_devices = lax.axis_size("zh"), lax.axis_size("zl")
    cols = block_cols.reshape(-1)
    z_of = cols % (zh_devices * zl_devices)
    cols = cols - z_of + (z_of % zl_devices) * zh_devices + z_of // zl_devices
    count = block_counts.reshape(-1)

    tile = (rows, cols, count, tile_blocks)
    sums_shape = (col_devices, width, nodes)

    def gather(value, axes):
        return lax.all_gather(value, axes, axis=0, tiled=False)

    def spread(along_zh):
        return to_all(along_zh, ("x", "zl")).reshape(row_devices, width, nodes)

    def reduce_core(partial):
        return exchange(partial.reshape(2, -1, nodes), "core").sum(0).reshape(y_devices, width, nodes)

    def reduce_y(chunks):
        return exchange(chunks, "y").sum(0) * scale

    def together(*values):
        return lax.optimization_barrier(values)

    def sum_to(chunks, copies):
        return call_kernel(sum_kernel, (chunks,), [(copies, *chunks.shape[1:])])[0]

    first = start.T
    along_zh, rider = together(to_all(first * scale, "zh"), gather(fold(gram(first, first)), COL))
    (partial,) = call_kernel(tile_kernel, (*tile, spread(along_zh)), [sums_shape])
    chunks, rider = together(reduce_core(partial), rider.sum(0))
    once, rider = together(reduce_y(chunks), gather(rider, "x"))

    rider = rider.sum(0).reshape(2, -1, nodes)
    half = rider.shape[1]
    rider = lax.dynamic_index_in_dim(rider, lax.axis_index("core"), keepdims=False)
    along_zh = to_all(jnp.concatenate([once * scale, rider], axis=0), "zh")
    gathered, rider = together(spread(along_zh[:, :width]), gather(along_zh[:, width:].sum(0), "core"))
    (partial,) = call_kernel(tile_kernel, (*tile, gathered), [sums_shape])
    chunks, rider = together(reduce_core(partial), rider.reshape(2 * half, nodes))
    (inverse,) = call_kernel(functools.partial(inverse_kernel, nodes_all), (gather(rider, "zl"),), [(width, width)])
    filtered = matmul(inverse, 2.0 * reduce_y(chunks) - first)

    scaled = filtered * scale
    along_zh, own_rows = together(to_all(scaled, "zh"), gather(scaled, COL))
    (projected,) = call_kernel(
        project_kernel,
        (*tile, spread(along_zh), own_rows, gram(filtered, filtered)),
        [(width, 2 * width)],
        [pltpu.VMEM(sums_shape, jnp.float32)],
    )
    projected = exchange(projected.reshape(col_devices, -1, 2 * width), COL)
    projected = exchange(sum_to(projected, row_devices), ROW)
    projected = exchange(sum_to(projected, col_devices), COL).reshape(width, 2 * width)
    basis, ritz = call_kernel(
        functools.partial(finish_kernel, nodes_all), (projected, filtered), [(width, nodes), (width, width)]
    )
    return (basis.T, ritz)


def solution(mesh):
    sizes = (4, 8, 2, 8, 2)
    return jax.shard_map(
        shards,
        mesh=Mesh(mesh.devices.reshape(sizes), AXES),
        in_specs=(
            P(AXES, None),
            P(AXES),
            P(ROW, COL, None, None, None),
            P(ROW, COL, None),
            P(ROW, COL, None),
            P(ROW, COL),
        ),
        out_specs=(P(AXES, None), P()),
        check_vma=False,
    )
```

```python
import functools

import jax
import jax.numpy as jnp
from jax import lax
from jax.experimental import pallas as pl
from jax.experimental.pallas import tpu as pltpu
from jax.sharding import Mesh, PartitionSpec as P

HIGHEST = lax.Precision.HIGHEST
AXES = ("x", "z", "y", "core")
ROW = ("x", "z")
COL = ("y", "core")
CONTRACT_LAST = (((1,), (1,)), ((), ()))


def exchange(chunks, axes):
    return lax.all_to_all(chunks, axes, 0, 0, tiled=True)


def to_all(value, axes):
    copies = lax.axis_size(axes)
    return exchange(jnp.broadcast_to(value[None], (copies, *value.shape)), axes)


def split(value):
    high = value.astype(jnp.bfloat16)
    return high, (value - high.astype(jnp.float32)).astype(jnp.bfloat16)


def dot_pieces(left, right):
    return lax.dot_general(left, right, CONTRACT_LAST, preferred_element_type=jnp.float32)


def add_slots(rows_ref, cols_ref, count_ref, blocks_ref, gathered_ref, sums_ref):
    sums_ref[...] = jnp.zeros_like(sums_ref)
    count = count_ref[0]
    width = sums_ref.shape[1]
    for slot in range(blocks_ref.shape[0]):
        live = (slot < count).astype(jnp.float32)
        high, low = split(gathered_ref[cols_ref[slot]] * live)
        block_high, block_low = split(blocks_ref[slot])
        both = dot_pieces(jnp.concatenate([high, low], axis=0), block_high)
        sums_ref[rows_ref[slot]] += both[:width] + both[width:] + dot_pieces(high, block_low)


def tile_kernel(rows_ref, cols_ref, count_ref, blocks_ref, gathered_ref, out_ref):
    add_slots(rows_ref, cols_ref, count_ref, blocks_ref, gathered_ref, out_ref)


def project_kernel(
    rows_ref, cols_ref, count_ref, blocks_ref, gathered_ref, own_ref, gram_ref, out_ref, sums_ref
):
    add_slots(rows_ref, cols_ref, count_ref, blocks_ref, gathered_ref, sums_ref)
    row_blocks, width, _ = sums_ref.shape
    half = row_blocks // 2
    products = jnp.zeros((2 * width, 2 * width), jnp.float32)
    for piece in range(row_blocks):
        left = jnp.concatenate(split(own_ref[piece]), axis=0)
        right = jnp.concatenate(split(sums_ref[(piece % 2) * half + piece // 2]), axis=0)
        products += dot_pieces(left, right)
    total = products[:width, :width] + products[:width, width:] + products[width:, :width] + products[width:, width:]
    out_ref[...] = jnp.concatenate([total, gram_ref[...]], axis=1)


def sum_kernel(chunks_ref, copies_ref):
    copies_ref[...] = jnp.broadcast_to(jnp.sum(chunks_ref[...], axis=0)[None], copies_ref.shape)


def inverse_factor(gram_matrix):
    size = gram_matrix.shape[0]
    shape = (size, 2 * size)
    row_of = lax.broadcasted_iota(jnp.int32, shape, 0)
    eye = (lax.broadcasted_iota(jnp.int32, (size, size), 0) == lax.broadcasted_iota(jnp.int32, (size, size), 1)).astype(
        jnp.float32
    )
    work = jnp.concatenate([gram_matrix, eye], axis=1)
    for j in range(0, size, 2):
        left = jnp.broadcast_to(work[:, j : j + 1], shape)
        right = jnp.broadcast_to(work[:, j + 1 : j + 2], shape)
        upper, lower = work[j : j + 1], work[j + 1 : j + 2]
        inverse_pivot = 1.0 / left[j : j + 1]
        ratio = left[j + 1 : j + 2] * inverse_pivot
        next_pivot = right[j + 1 : j + 2] - ratio * left[j + 1 : j + 2]
        lower = (lower - ratio * upper) * (1.0 / next_pivot)
        right = jnp.where(row_of > j + 1, right - left * ratio, 0.0)
        left = jnp.where(row_of > j, left, 0.0)
        work = work - left * (upper * inverse_pivot) - right * lower
    diagonal = jnp.sum(work[:, :size] * eye, axis=1, keepdims=True)
    return work[:, size:] * lax.rsqrt(diagonal)


def inverse_kernel(nodes_all, folded_ref, out_ref):
    out_ref[...] = inverse_factor(unfold(folded_ref[...]) / nodes_all)


def finish_kernel(nodes_all, both_ref, filtered_ref, basis_ref, ritz_ref):
    width = filtered_ref.shape[0]
    both = both_ref[...] / nodes_all
    inverse = inverse_factor(both[:, width:])
    half = jnp.dot(inverse, both[:, :width], precision=HIGHEST, preferred_element_type=jnp.float32)
    ritz_ref[...] = lax.dot_general(
        half, inverse, CONTRACT_LAST, precision=HIGHEST, preferred_element_type=jnp.float32
    )
    basis_ref[...] = jnp.dot(inverse, filtered_ref[...], precision=HIGHEST, preferred_element_type=jnp.float32)


SMEM = pl.BlockSpec(memory_space=pltpu.SMEM)
VMEM = pl.BlockSpec(memory_space=pltpu.VMEM)


def call_kernel(kernel, ins, outs, scratch=()):
    return pl.pallas_call(
        kernel,
        out_shape=[jax.ShapeDtypeStruct(shape, jnp.float32) for shape in outs],
        in_specs=[SMEM if value.dtype == jnp.int32 else VMEM for value in ins],
        out_specs=[VMEM] * len(outs),
        scratch_shapes=list(scratch),
        compiler_params=pltpu.CompilerParams(vmem_limit_bytes=24 * 2**20),
    )(*ins)


def gram(left, right):
    return lax.dot_general(left, right, CONTRACT_LAST, precision=HIGHEST)


def matmul(left, right):
    return jnp.dot(left, right, precision=HIGHEST)


def fold(square):
    half = square.shape[0] // 2
    return jnp.concatenate([square[:half], square[half:]], axis=1)


def unfold(folded):
    half = folded.shape[1] // 2
    return jnp.concatenate([folded[:, :half], folded[:, half:]], axis=0)


def shards(start, degrees, blocks, block_rows, block_cols, block_counts):
    row_devices = lax.axis_size(ROW)
    col_devices = lax.axis_size(COL)
    nodes, width = start.shape
    nodes_all = nodes * row_devices * col_devices
    scale = jnp.sqrt(16.0 / degrees.astype(jnp.float32))[None, :]
    tile_blocks = blocks.reshape(blocks.shape[2:])
    rows = block_rows.reshape(-1)
    y_devices = lax.axis_size("y")
    rows = (rows % 2) * y_devices + rows // 2
    cols = block_cols.reshape(-1)
    count = block_counts.reshape(-1)

    tile = (rows, cols, count, tile_blocks)
    sums_shape = (col_devices, width, nodes)

    def gather(value, axes):
        return lax.all_gather(value, axes, axis=0, tiled=False)

    def spread(along_z):
        return to_all(along_z, "x").reshape(row_devices, width, nodes)

    def reduce_core(partial):
        return exchange(partial.reshape(2, -1, nodes), "core").sum(0).reshape(y_devices, width, nodes)

    def reduce_y(chunks):
        return exchange(chunks, "y").sum(0) * scale

    def together(*values):
        return lax.optimization_barrier(values)

    def sum_to(chunks, copies):
        return call_kernel(sum_kernel, (chunks,), [(copies, *chunks.shape[1:])])[0]

    first = start.T
    along_z = gather(first * scale, "z")
    gathered, rider = together(spread(along_z), gather(fold(gram(first, first)), COL))
    (partial,) = call_kernel(tile_kernel, (*tile, gathered), [sums_shape])
    chunks, rider = together(reduce_core(partial), rider.sum(0))
    once, rider = together(reduce_y(chunks), gather(rider, "x"))

    rider = rider.sum(0).reshape(2, -1, nodes)
    half = rider.shape[1]
    rider = lax.dynamic_index_in_dim(rider, lax.axis_index("core"), keepdims=False)
    along_z = gather(jnp.concatenate([once * scale, rider], axis=0), "z")
    gathered, rider = together(spread(along_z[:, :width]), gather(along_z[:, width:].sum(0), "core"))
    (partial,) = call_kernel(tile_kernel, (*tile, gathered), [sums_shape])
    chunks, rider = together(reduce_core(partial), rider.reshape(2 * half, nodes))
    (inverse,) = call_kernel(functools.partial(inverse_kernel, nodes_all), (rider,), [(width, width)])
    filtered = matmul(inverse, 2.0 * reduce_y(chunks) - first)

    scaled = filtered * scale
    gathered, own_rows = together(spread(gather(scaled, "z")), gather(scaled, COL))
    (projected,) = call_kernel(
        project_kernel,
        (*tile, gathered, own_rows, gram(filtered, filtered)),
        [(width, 2 * width)],
        [pltpu.VMEM(sums_shape, jnp.float32)],
    )
    projected = exchange(projected.reshape(col_devices, -1, 2 * width), COL)
    projected = exchange(sum_to(projected, row_devices), ROW)
    projected = exchange(sum_to(projected, col_devices), COL).reshape(width, 2 * width)
    basis, ritz = call_kernel(
        functools.partial(finish_kernel, nodes_all), (projected, filtered), [(width, nodes), (width, width)]
    )
    return (basis.T, ritz)


def solution(mesh):
    sizes = (4, 16, 8, 2)
    return jax.shard_map(
        shards,
        mesh=Mesh(mesh.devices.reshape(sizes), AXES),
        in_specs=(
            P(AXES, None),
            P(AXES),
            P(ROW, COL, None, None, None),
            P(ROW, COL, None),
            P(ROW, COL, None),
            P(ROW, COL),
        ),
        out_specs=(P(AXES, None), P()),
        check_vma=False,
    )
```

```python
import functools

import jax
import jax.numpy as jnp
from jax import lax
from jax.experimental import pallas as pl
from jax.experimental.pallas import tpu as pltpu
from jax.sharding import Mesh, PartitionSpec as P

HIGHEST = lax.Precision.HIGHEST
AXES = ("x", "za", "zb", "y", "core")
ROW = ("x", "za", "zb")
COL = ("y", "core")
CONTRACT_LAST = (((1,), (1,)), ((), ()))


def exchange(chunks, axes):
    return lax.all_to_all(chunks, axes, 0, 0, tiled=True)


def to_all(value, axes):
    copies = lax.axis_size(axes)
    return exchange(jnp.broadcast_to(value[None], (copies, *value.shape)), axes)


def split(value):
    high = value.astype(jnp.bfloat16)
    return high, (value - high.astype(jnp.float32)).astype(jnp.bfloat16)


def dot_pieces(left, right):
    return lax.dot_general(left, right, CONTRACT_LAST, preferred_element_type=jnp.float32)


def add_slots(rows_ref, cols_ref, count_ref, blocks_ref, gathered_ref, sums_ref):
    sums_ref[...] = jnp.zeros_like(sums_ref)
    count = count_ref[0]
    width = sums_ref.shape[1]
    for slot in range(blocks_ref.shape[0]):
        live = (slot < count).astype(jnp.float32)
        high, low = split(gathered_ref[cols_ref[slot]] * live)
        block_high, block_low = split(blocks_ref[slot])
        both = dot_pieces(jnp.concatenate([high, low], axis=0), block_high)
        sums_ref[rows_ref[slot]] += both[:width] + both[width:] + dot_pieces(high, block_low)


def tile_kernel(rows_ref, cols_ref, count_ref, blocks_ref, gathered_ref, out_ref):
    add_slots(rows_ref, cols_ref, count_ref, blocks_ref, gathered_ref, out_ref)


def project_kernel(
    rows_ref, cols_ref, count_ref, blocks_ref, gathered_ref, own_ref, gram_ref, out_ref, sums_ref
):
    add_slots(rows_ref, cols_ref, count_ref, blocks_ref, gathered_ref, sums_ref)
    row_blocks, width, _ = sums_ref.shape
    half = row_blocks // 2
    products = jnp.zeros((2 * width, 2 * width), jnp.float32)
    for piece in range(row_blocks):
        left = jnp.concatenate(split(own_ref[piece]), axis=0)
        right = jnp.concatenate(split(sums_ref[(piece % 2) * half + piece // 2]), axis=0)
        products += dot_pieces(left, right)
    total = products[:width, :width] + products[:width, width:] + products[width:, :width] + products[width:, width:]
    out_ref[...] = jnp.concatenate([total, gram_ref[...]], axis=1)


def sum_kernel(chunks_ref, copies_ref):
    copies_ref[...] = jnp.broadcast_to(jnp.sum(chunks_ref[...], axis=0)[None], copies_ref.shape)


def inverse_factor(gram_matrix):
    size = gram_matrix.shape[0]
    shape = (size, 2 * size)
    row_of = lax.broadcasted_iota(jnp.int32, shape, 0)
    eye = (lax.broadcasted_iota(jnp.int32, (size, size), 0) == lax.broadcasted_iota(jnp.int32, (size, size), 1)).astype(
        jnp.float32
    )
    work = jnp.concatenate([gram_matrix, eye], axis=1)
    for j in range(0, size, 2):
        left = jnp.broadcast_to(work[:, j : j + 1], shape)
        right = jnp.broadcast_to(work[:, j + 1 : j + 2], shape)
        upper, lower = work[j : j + 1], work[j + 1 : j + 2]
        inverse_pivot = 1.0 / left[j : j + 1]
        ratio = left[j + 1 : j + 2] * inverse_pivot
        next_pivot = right[j + 1 : j + 2] - ratio * left[j + 1 : j + 2]
        lower = (lower - ratio * upper) * (1.0 / next_pivot)
        right = jnp.where(row_of > j + 1, right - left * ratio, 0.0)
        left = jnp.where(row_of > j, left, 0.0)
        work = work - left * (upper * inverse_pivot) - right * lower
    diagonal = jnp.sum(work[:, :size] * eye, axis=1, keepdims=True)
    return work[:, size:] * lax.rsqrt(diagonal)


def inverse_kernel(nodes_all, folded_ref, out_ref):
    out_ref[...] = inverse_factor(unfold(folded_ref[...]) / nodes_all)


def finish_kernel(nodes_all, both_ref, filtered_ref, basis_ref, ritz_ref):
    width = filtered_ref.shape[0]
    both = both_ref[...] / nodes_all
    inverse = inverse_factor(both[:, width:])
    half = jnp.dot(inverse, both[:, :width], precision=HIGHEST, preferred_element_type=jnp.float32)
    ritz_ref[...] = lax.dot_general(
        half, inverse, CONTRACT_LAST, precision=HIGHEST, preferred_element_type=jnp.float32
    )
    basis_ref[...] = jnp.dot(inverse, filtered_ref[...], precision=HIGHEST, preferred_element_type=jnp.float32)


SMEM = pl.BlockSpec(memory_space=pltpu.SMEM)
VMEM = pl.BlockSpec(memory_space=pltpu.VMEM)


def call_kernel(kernel, ins, outs, scratch=()):
    return pl.pallas_call(
        kernel,
        out_shape=[jax.ShapeDtypeStruct(shape, jnp.float32) for shape in outs],
        in_specs=[SMEM if value.dtype == jnp.int32 else VMEM for value in ins],
        out_specs=[VMEM] * len(outs),
        scratch_shapes=list(scratch),
        compiler_params=pltpu.CompilerParams(vmem_limit_bytes=24 * 2**20),
    )(*ins)


def gram(left, right):
    return lax.dot_general(left, right, CONTRACT_LAST, precision=HIGHEST)


def matmul(left, right):
    return jnp.dot(left, right, precision=HIGHEST)


def fold(square):
    half = square.shape[0] // 2
    return jnp.concatenate([square[:half], square[half:]], axis=1)


def unfold(folded):
    half = folded.shape[1] // 2
    return jnp.concatenate([folded[:, :half], folded[:, half:]], axis=0)


def shards(start, degrees, blocks, block_rows, block_cols, block_counts):
    row_devices = lax.axis_size(ROW)
    col_devices = lax.axis_size(COL)
    nodes, width = start.shape
    nodes_all = nodes * row_devices * col_devices
    scale = jnp.sqrt(16.0 / degrees.astype(jnp.float32))[None, :]
    tile_blocks = blocks.reshape(blocks.shape[2:])
    rows = block_rows.reshape(-1)
    y_devices = lax.axis_size("y")
    rows = (rows % 2) * y_devices + rows // 2
    za_devices, zb_devices = lax.axis_size("za"), lax.axis_size("zb")
    cols = block_cols.reshape(-1)
    z_of = cols % (za_devices * zb_devices)
    cols = cols - z_of + (z_of % zb_devices) * za_devices + z_of // zb_devices
    count = block_counts.reshape(-1)

    tile = (rows, cols, count, tile_blocks)
    sums_shape = (col_devices, width, nodes)

    def gather(value, axes):
        return lax.all_gather(value, axes, axis=0, tiled=False)

    def gather_z(value):
        along_z = gather(gather(value, "za"), "zb")
        return along_z.reshape(-1, *value.shape)

    def spread(along_z):
        return to_all(along_z, "x").reshape(row_devices, width, nodes)

    def reduce_core(partial):
        return exchange(partial.reshape(2, -1, nodes), "core").sum(0).reshape(y_devices, width, nodes)

    def reduce_y(chunks):
        return exchange(chunks, "y").sum(0) * scale

    def together(*values):
        return lax.optimization_barrier(values)

    def sum_to(chunks, copies):
        return call_kernel(sum_kernel, (chunks,), [(copies, *chunks.shape[1:])])[0]

    first = start.T
    along_z = gather_z(first * scale)
    gathered, rider = together(spread(along_z), gather(fold(gram(first, first)), COL))
    (partial,) = call_kernel(tile_kernel, (*tile, gathered), [sums_shape])
    chunks, rider = together(reduce_core(partial), rider.sum(0))
    once, rider = together(reduce_y(chunks), gather(rider, "x"))

    rider = rider.sum(0).reshape(2, -1, nodes)
    half = rider.shape[1]
    rider = lax.dynamic_index_in_dim(rider, lax.axis_index("core"), keepdims=False)
    along_z = gather_z(jnp.concatenate([once * scale, rider], axis=0))
    gathered, rider = together(spread(along_z[:, :width]), gather(along_z[:, width:].sum(0), "core"))
    (partial,) = call_kernel(tile_kernel, (*tile, gathered), [sums_shape])
    chunks, rider = together(reduce_core(partial), rider.reshape(2 * half, nodes))
    (inverse,) = call_kernel(functools.partial(inverse_kernel, nodes_all), (rider,), [(width, width)])
    filtered = matmul(inverse, 2.0 * reduce_y(chunks) - first)

    scaled = filtered * scale
    gathered, own_rows = together(spread(gather_z(scaled)), gather(scaled, COL))
    (projected,) = call_kernel(
        project_kernel,
        (*tile, gathered, own_rows, gram(filtered, filtered)),
        [(width, 2 * width)],
        [pltpu.VMEM(sums_shape, jnp.float32)],
    )
    projected = exchange(projected.reshape(col_devices, -1, 2 * width), COL)
    projected = exchange(sum_to(projected, row_devices), ROW)
    projected = exchange(sum_to(projected, col_devices), COL).reshape(width, 2 * width)
    basis, ritz = call_kernel(
        functools.partial(finish_kernel, nodes_all), (projected, filtered), [(width, nodes), (width, width)]
    )
    return (basis.T, ritz)


def solution(mesh):
    sizes = (4, 4, 4, 8, 2)
    return jax.shard_map(
        shards,
        mesh=Mesh(mesh.devices.reshape(sizes), AXES),
        in_specs=(
            P(AXES, None),
            P(AXES),
            P(ROW, COL, None, None, None),
            P(ROW, COL, None),
            P(ROW, COL, None),
            P(ROW, COL),
        ),
        out_specs=(P(AXES, None), P()),
        check_vma=False,
    )
```

```python
import functools

import jax
import jax.numpy as jnp
from jax import lax
from jax.experimental import pallas as pl
from jax.experimental.pallas import tpu as pltpu
from jax.sharding import Mesh, PartitionSpec as P

HIGHEST = lax.Precision.HIGHEST
AXES = ("x", "z", "y", "core")
ROW = ("x", "z")
COL = ("y", "core")
CONTRACT_LAST = (((1,), (1,)), ((), ()))


def exchange(chunks, axes):
    return lax.all_to_all(chunks, axes, 0, 0, tiled=True)


def to_all(value, axes):
    copies = lax.axis_size(axes)
    return exchange(jnp.broadcast_to(value[None], (copies, *value.shape)), axes)


def split(value):
    high = value.astype(jnp.bfloat16)
    return high, (value - high.astype(jnp.float32)).astype(jnp.bfloat16)


def dot_pieces(left, right):
    return lax.dot_general(left, right, CONTRACT_LAST, preferred_element_type=jnp.float32)


def add_slots(rows_ref, cols_ref, count_ref, blocks_ref, gathered_ref, sums_ref):
    sums_ref[...] = jnp.zeros_like(sums_ref)
    count = count_ref[0]
    width = sums_ref.shape[1]
    pieces = gathered_ref.shape[1] // width
    for slot in range(blocks_ref.shape[0]):
        live = (slot < count).astype(jnp.float32)
        col = cols_ref[slot]
        first_row = pl.multiple_of((col % pieces) * width, width)
        high, low = split(gathered_ref[col // pieces, pl.ds(first_row, width)] * live)
        block_high, block_low = split(blocks_ref[slot])
        both = dot_pieces(jnp.concatenate([high, low], axis=0), block_high)
        sums_ref[rows_ref[slot]] += both[:width] + both[width:] + dot_pieces(high, block_low)


def tile_kernel(rows_ref, cols_ref, count_ref, blocks_ref, gathered_ref, out_ref):
    add_slots(rows_ref, cols_ref, count_ref, blocks_ref, gathered_ref, out_ref)


def tile_rider_kernel(rows_ref, cols_ref, count_ref, blocks_ref, gathered_ref, out_ref, rider_ref):
    add_slots(rows_ref, cols_ref, count_ref, blocks_ref, gathered_ref, out_ref)
    pieces_end = gathered_ref.shape[1] - rider_ref.shape[0]
    rider_ref[...] = jnp.sum(gathered_ref[:, pieces_end:], axis=0)


def scale_kernel(degrees_hbm, vectors_hbm, scale_ref, scaled_ref, degrees_ref, vectors_ref, sems):
    fetches = [
        pltpu.make_async_copy(degrees_hbm, degrees_ref, sems.at[0]),
        pltpu.make_async_copy(vectors_hbm, vectors_ref, sems.at[1]),
    ]
    for fetch in fetches:
        fetch.start()
    for fetch in fetches:
        fetch.wait()
    scale = jnp.sqrt(16.0 / degrees_ref[...].astype(jnp.float32))
    scale_ref[...] = scale
    scaled_ref[...] = vectors_ref[...] * scale


def project_kernel(
    rows_ref, cols_ref, count_ref, blocks_ref, gathered_ref, own_ref, gram_ref, out_ref, sums_ref
):
    add_slots(rows_ref, cols_ref, count_ref, blocks_ref, gathered_ref, sums_ref)
    row_blocks, width, _ = sums_ref.shape
    products = jnp.zeros((2 * width, 2 * width), jnp.float32)
    for piece in range(row_blocks):
        left = jnp.concatenate(split(own_ref[piece]), axis=0)
        right = jnp.concatenate(split(sums_ref[piece]), axis=0)
        products += dot_pieces(left, right)
    total = products[:width, :width] + products[:width, width:] + products[width:, :width] + products[width:, width:]
    out_ref[...] = jnp.concatenate([total, gram_ref[...]], axis=1)


def sum_kernel(chunks_ref, copies_ref):
    copies_ref[...] = jnp.broadcast_to(jnp.sum(chunks_ref[...], axis=0)[None], copies_ref.shape)


def inverse_factor(gram_matrix):
    size = gram_matrix.shape[0]
    shape = (size, 2 * size)
    row_of = lax.broadcasted_iota(jnp.int32, shape, 0)
    eye = (lax.broadcasted_iota(jnp.int32, (size, size), 0) == lax.broadcasted_iota(jnp.int32, (size, size), 1)).astype(
        jnp.float32
    )
    work = jnp.concatenate([gram_matrix, eye], axis=1)
    for j in range(0, size, 2):
        left = jnp.broadcast_to(work[:, j : j + 1], shape)
        right = jnp.broadcast_to(work[:, j + 1 : j + 2], shape)
        upper, lower = work[j : j + 1], work[j + 1 : j + 2]
        inverse_pivot = 1.0 / left[j : j + 1]
        ratio = left[j + 1 : j + 2] * inverse_pivot
        next_pivot = right[j + 1 : j + 2] - ratio * left[j + 1 : j + 2]
        lower = (lower - ratio * upper) * (1.0 / next_pivot)
        right = jnp.where(row_of > j + 1, right - left * ratio, 0.0)
        left = jnp.where(row_of > j, left, 0.0)
        work = work - left * (upper * inverse_pivot) - right * lower
    diagonal = jnp.sum(work[:, :size] * eye, axis=1, keepdims=True)
    return work[:, size:] * lax.rsqrt(diagonal)


def inverse_kernel(nodes_all, folded_ref, out_ref):
    out_ref[...] = inverse_factor(unfold(folded_ref[...]) / nodes_all)


def finish_kernel(nodes_all, both_ref, filtered_ref, basis_ref, ritz_ref):
    width = filtered_ref.shape[0]
    both = both_ref[...] / nodes_all
    inverse = inverse_factor(both[:, width:])
    half = jnp.dot(inverse, both[:, :width], precision=HIGHEST, preferred_element_type=jnp.float32)
    ritz_ref[...] = lax.dot_general(
        half, inverse, CONTRACT_LAST, precision=HIGHEST, preferred_element_type=jnp.float32
    )
    basis_ref[...] = jnp.dot(inverse, filtered_ref[...], precision=HIGHEST, preferred_element_type=jnp.float32)


SMEM = pl.BlockSpec(memory_space=pltpu.SMEM)
VMEM = pl.BlockSpec(memory_space=pltpu.VMEM)
HBM = pl.BlockSpec(memory_space=pltpu.HBM)


def call_kernel(kernel, ins, outs, scratch=(), in_specs=None):
    return pl.pallas_call(
        kernel,
        out_shape=[jax.ShapeDtypeStruct(shape, jnp.float32) for shape in outs],
        in_specs=in_specs
        or [SMEM if value.dtype == jnp.int32 and value.ndim == 1 else VMEM for value in ins],
        out_specs=[VMEM] * len(outs),
        scratch_shapes=list(scratch),
        compiler_params=pltpu.CompilerParams(vmem_limit_bytes=24 * 2**20),
    )(*ins)


def gram(left, right):
    return lax.dot_general(left, right, CONTRACT_LAST, precision=HIGHEST)


def matmul(left, right):
    return jnp.dot(left, right, precision=HIGHEST)


def fold(square):
    half = square.shape[0] // 2
    return jnp.concatenate([square[:half], square[half:]], axis=1)


def unfold(folded):
    half = folded.shape[1] // 2
    return jnp.concatenate([folded[:, :half], folded[:, half:]], axis=0)


def shards(start, degrees, blocks, block_rows, block_cols, block_counts):
    row_devices = lax.axis_size(ROW)
    col_devices = lax.axis_size(COL)
    nodes, width = start.shape
    nodes_all = nodes * row_devices * col_devices
    tile_blocks = blocks.reshape(blocks.shape[2:])
    rows = block_rows.reshape(-1)
    cols = block_cols.reshape(-1)
    count = block_counts.reshape(-1)

    tile = (rows, cols, count, tile_blocks)
    sums_shape = (col_devices, width, nodes)

    def gather(value, axes):
        return lax.all_gather(value, axes, axis=0, tiled=False)

    def reduce_cols(partial):
        along_y = exchange(partial.reshape(lax.axis_size("y"), -1, nodes), "y").sum(0)
        return exchange(along_y.reshape(lax.axis_size("core"), width, nodes), "core").sum(0) * scale

    def together(*values):
        return lax.optimization_barrier(values)

    def sum_to(chunks, copies):
        return call_kernel(sum_kernel, (chunks,), [(copies, *chunks.shape[1:])])[0]

    first = start.T
    scale, scaled = call_kernel(
        scale_kernel,
        (degrees[None], first),
        [(1, nodes), (width, nodes)],
        [pltpu.VMEM((1, nodes), jnp.int32), pltpu.VMEM((width, nodes), jnp.float32), pltpu.SemaphoreType.DMA((2,))],
        [HBM, HBM],
    )
    along_z = gather(scaled, "z").reshape(-1, nodes)
    rider = gather(fold(gram(first, first)), COL).sum(0).reshape(lax.axis_size("core"), -1, nodes)
    half_shape = rider.shape[1:]
    rider = lax.dynamic_index_in_dim(rider, lax.axis_index("core"), keepdims=False)
    gathered, rider = together(to_all(along_z, "x"), rider)
    (partial,) = call_kernel(tile_kernel, (*tile, gathered), [sums_shape])
    once = reduce_cols(partial)

    along_z = gather(jnp.concatenate([once * scale, rider], axis=0), "z")
    along_z = jnp.concatenate([along_z[:, :width].reshape(-1, nodes), along_z[:, width:].sum(0)], axis=0)
    partial, rider = call_kernel(tile_rider_kernel, (*tile, to_all(along_z, "x")), [sums_shape, half_shape])
    rider = gather(rider, "core").reshape(-1, nodes)
    (inverse,) = call_kernel(functools.partial(inverse_kernel, nodes_all), (rider,), [(width, width)])
    filtered = matmul(inverse, 2.0 * reduce_cols(partial) - first)

    scaled = filtered * scale
    gathered, own_rows = together(to_all(gather(scaled, "z").reshape(-1, nodes), "x"), gather(scaled, COL))
    (projected,) = call_kernel(
        project_kernel,
        (*tile, gathered, own_rows, gram(filtered, filtered)),
        [(width, 2 * width)],
        [pltpu.VMEM(sums_shape, jnp.float32)],
    )
    projected = exchange(projected.reshape(col_devices, -1, 2 * width), COL)
    projected = exchange(sum_to(projected, row_devices), ROW)
    projected = exchange(sum_to(projected, col_devices), COL).reshape(width, 2 * width)
    basis, ritz = call_kernel(
        functools.partial(finish_kernel, nodes_all), (projected, filtered), [(width, nodes), (width, width)]
    )
    return (basis.T, ritz)


def solution(mesh):
    sizes = (4, 16, 8, 2)
    return jax.shard_map(
        shards,
        mesh=Mesh(mesh.devices.reshape(sizes), AXES),
        in_specs=(
            P(AXES, None),
            P(AXES),
            P(ROW, COL, None, None, None),
            P(ROW, COL, None),
            P(ROW, COL, None),
            P(ROW, COL),
        ),
        out_specs=(P(AXES, None), P()),
        check_vma=False,
    )
```

```python
import functools

import jax
import jax.numpy as jnp
from jax import lax
from jax.experimental import pallas as pl
from jax.experimental.pallas import tpu as pltpu
from jax.sharding import Mesh, PartitionSpec as P

HIGHEST = lax.Precision.HIGHEST
AXES = ("x", "z", "y", "core")
ROW = ("x", "z")
COL = ("y", "core")
CONTRACT_LAST = (((1,), (1,)), ((), ()))


def exchange(chunks, axes):
    return lax.all_to_all(chunks, axes, 0, 0, tiled=True)


def to_all(value, axes):
    copies = lax.axis_size(axes)
    return exchange(jnp.broadcast_to(value[None], (copies, *value.shape)), axes)


def split(value):
    high = value.astype(jnp.bfloat16)
    return high, (value - high.astype(jnp.float32)).astype(jnp.bfloat16)


def dot_pieces(left, right):
    return lax.dot_general(left, right, CONTRACT_LAST, preferred_element_type=jnp.float32)


def add_slots(rows_ref, cols_ref, count_ref, blocks_ref, gathered_ref, sums_ref):
    sums_ref[...] = jnp.zeros_like(sums_ref)
    count = count_ref[0]
    width, nodes = sums_ref.shape[1:]
    pieces = gathered_ref.shape[1] // width
    for slot in range(blocks_ref.shape[0]):
        live = (slot < count).astype(jnp.float32)
        col = cols_ref[slot]
        first_row = pl.multiple_of((col % pieces) * width, width)
        vectors = jnp.concatenate(split(gathered_ref[col // pieces, pl.ds(first_row, width)] * live), axis=0)
        products = dot_pieces(vectors, jnp.concatenate(split(blocks_ref[slot]), axis=0))
        sums_ref[rows_ref[slot]] += products[:width, :nodes] + products[width:, :nodes] + products[:width, nodes:]


def tile_kernel(rows_ref, cols_ref, count_ref, blocks_ref, gathered_ref, out_ref):
    add_slots(rows_ref, cols_ref, count_ref, blocks_ref, gathered_ref, out_ref)


def tile_rider_kernel(rows_ref, cols_ref, count_ref, blocks_ref, gathered_ref, out_ref, rider_ref):
    add_slots(rows_ref, cols_ref, count_ref, blocks_ref, gathered_ref, out_ref)
    pieces_end = gathered_ref.shape[1] - rider_ref.shape[0]
    rider_ref[...] = jnp.sum(gathered_ref[:, pieces_end:], axis=0)


def scale_kernel(degrees_hbm, vectors_hbm, scale_ref, scaled_ref, degrees_ref, vectors_ref, sems):
    fetches = [
        pltpu.make_async_copy(degrees_hbm, degrees_ref, sems.at[0]),
        pltpu.make_async_copy(vectors_hbm, vectors_ref, sems.at[1]),
    ]
    for fetch in fetches:
        fetch.start()
    for fetch in fetches:
        fetch.wait()
    scale = jnp.sqrt(16.0 / degrees_ref[...].astype(jnp.float32))
    scale_ref[...] = scale
    scaled_ref[...] = vectors_ref[...] * scale


def project_kernel(
    rows_ref, cols_ref, count_ref, blocks_ref, gathered_ref, own_ref, gram_ref, out_ref, sums_ref
):
    add_slots(rows_ref, cols_ref, count_ref, blocks_ref, gathered_ref, sums_ref)
    row_blocks, width, _ = sums_ref.shape
    products = jnp.zeros((2 * width, 2 * width), jnp.float32)
    for piece in range(row_blocks):
        left = jnp.concatenate(split(own_ref[piece]), axis=0)
        right = jnp.concatenate(split(sums_ref[piece]), axis=0)
        products += dot_pieces(left, right)
    total = products[:width, :width] + products[:width, width:] + products[width:, :width] + products[width:, width:]
    out_ref[...] = jnp.concatenate([total, gram_ref[...]], axis=1)


def sum_kernel(chunks_ref, copies_ref):
    copies_ref[...] = jnp.broadcast_to(jnp.sum(chunks_ref[...], axis=0)[None], copies_ref.shape)


def inverse_factor(gram_matrix, pivots=4):
    size = gram_matrix.shape[0]
    shape = (size, 2 * size)
    row_of = lax.broadcasted_iota(jnp.int32, shape, 0)
    eye = (lax.broadcasted_iota(jnp.int32, (size, size), 0) == lax.broadcasted_iota(jnp.int32, (size, size), 1)).astype(
        jnp.float32
    )
    work = jnp.concatenate([gram_matrix, eye], axis=1)
    for first in range(0, size, pivots):
        columns = [jnp.broadcast_to(work[:, j : j + 1], shape) for j in range(first, first + pivots)]
        upper = [work[j : j + 1] for j in range(first, first + pivots)]
        taken = jnp.zeros(shape, jnp.float32)
        for k in range(pivots):
            inverse_pivot = 1.0 / columns[k][first + k : first + k + 1]
            upper[k] = upper[k] * inverse_pivot
            for m in range(k + 1, pivots):
                factor = columns[k][first + m : first + m + 1]
                upper[m] = upper[m] - factor * upper[k]
                columns[m] = columns[m] - columns[k] * (factor * inverse_pivot)
            taken += jnp.where(row_of > first + k, columns[k], 0.0) * upper[k]
        work = work - taken
    diagonal = jnp.sum(work[:, :size] * eye, axis=1, keepdims=True)
    return work[:, size:] * lax.rsqrt(diagonal)


def inverse_kernel(nodes_all, folded_ref, out_ref):
    out_ref[...] = inverse_factor(unfold(folded_ref[...]) / nodes_all)


def finish_kernel(nodes_all, both_ref, filtered_ref, basis_ref, ritz_ref):
    width = filtered_ref.shape[0]
    both = both_ref[...] / nodes_all
    inverse = inverse_factor(both[:, width:])
    half = jnp.dot(inverse, both[:, :width], precision=HIGHEST, preferred_element_type=jnp.float32)
    ritz_ref[...] = lax.dot_general(
        half, inverse, CONTRACT_LAST, precision=HIGHEST, preferred_element_type=jnp.float32
    )
    basis_ref[...] = jnp.dot(inverse, filtered_ref[...], precision=HIGHEST, preferred_element_type=jnp.float32)


SMEM = pl.BlockSpec(memory_space=pltpu.SMEM)
VMEM = pl.BlockSpec(memory_space=pltpu.VMEM)
HBM = pl.BlockSpec(memory_space=pltpu.HBM)


def call_kernel(kernel, ins, outs, scratch=(), in_specs=None):
    return pl.pallas_call(
        kernel,
        out_shape=[jax.ShapeDtypeStruct(shape, jnp.float32) for shape in outs],
        in_specs=in_specs
        or [SMEM if value.dtype == jnp.int32 and value.ndim == 1 else VMEM for value in ins],
        out_specs=[VMEM] * len(outs),
        scratch_shapes=list(scratch),
        compiler_params=pltpu.CompilerParams(vmem_limit_bytes=24 * 2**20),
    )(*ins)


def gram(left, right):
    return lax.dot_general(left, right, CONTRACT_LAST, precision=HIGHEST)


def matmul(left, right):
    return jnp.dot(left, right, precision=HIGHEST)


def fold(square):
    half = square.shape[0] // 2
    return jnp.concatenate([square[:half], square[half:]], axis=1)


def unfold(folded):
    half = folded.shape[1] // 2
    return jnp.concatenate([folded[:, :half], folded[:, half:]], axis=0)


def shards(start, degrees, blocks, block_rows, block_cols, block_counts):
    row_devices = lax.axis_size(ROW)
    col_devices = lax.axis_size(COL)
    nodes, width = start.shape
    nodes_all = nodes * row_devices * col_devices
    tile_blocks = blocks.reshape(blocks.shape[2:])
    rows = block_rows.reshape(-1)
    cols = block_cols.reshape(-1)
    count = block_counts.reshape(-1)

    tile = (rows, cols, count, tile_blocks)
    sums_shape = (col_devices, width, nodes)

    def gather(value, axes):
        return lax.all_gather(value, axes, axis=0, tiled=False)

    def reduce_cols(partial):
        along_y = exchange(partial.reshape(lax.axis_size("y"), -1, nodes), "y").sum(0)
        return exchange(along_y.reshape(lax.axis_size("core"), width, nodes), "core").sum(0) * scale

    def together(*values):
        return lax.optimization_barrier(values)

    def sum_to(chunks, copies):
        return call_kernel(sum_kernel, (chunks,), [(copies, *chunks.shape[1:])])[0]

    first = start.T
    scale, scaled = call_kernel(
        scale_kernel,
        (degrees[None], first),
        [(1, nodes), (width, nodes)],
        [pltpu.VMEM((1, nodes), jnp.int32), pltpu.VMEM((width, nodes), jnp.float32), pltpu.SemaphoreType.DMA((2,))],
        [HBM, HBM],
    )
    along_z = gather(scaled, "z").reshape(-1, nodes)
    rider = gather(fold(gram(first, first)), COL).sum(0).reshape(lax.axis_size("core"), -1, nodes)
    half_shape = rider.shape[1:]
    rider = lax.dynamic_index_in_dim(rider, lax.axis_index("core"), keepdims=False)
    gathered, rider = together(to_all(along_z, "x"), rider)
    (partial,) = call_kernel(tile_kernel, (*tile, gathered), [sums_shape])
    once = reduce_cols(partial)

    along_z = gather(jnp.concatenate([once * scale, rider], axis=0), "z")
    along_z = jnp.concatenate([along_z[:, :width].reshape(-1, nodes), along_z[:, width:].sum(0)], axis=0)
    partial, rider = call_kernel(tile_rider_kernel, (*tile, to_all(along_z, "x")), [sums_shape, half_shape])
    rider = gather(rider, "core").reshape(-1, nodes)
    (inverse,) = call_kernel(functools.partial(inverse_kernel, nodes_all), (rider,), [(width, width)])
    filtered = matmul(inverse, 2.0 * reduce_cols(partial) - first)

    scaled = filtered * scale
    gathered, own_rows = together(to_all(gather(scaled, "z").reshape(-1, nodes), "x"), gather(scaled, COL))
    (projected,) = call_kernel(
        project_kernel,
        (*tile, gathered, own_rows, gram(filtered, filtered)),
        [(width, 2 * width)],
        [pltpu.VMEM(sums_shape, jnp.float32)],
    )
    projected = exchange(projected.reshape(col_devices, -1, 2 * width), COL)
    projected = exchange(sum_to(projected, row_devices), ROW)
    projected = exchange(sum_to(projected, col_devices), COL).reshape(width, 2 * width)
    basis, ritz = call_kernel(
        functools.partial(finish_kernel, nodes_all), (projected, filtered), [(width, nodes), (width, width)]
    )
    return (basis.T, ritz)


def solution(mesh):
    sizes = (4, 16, 8, 2)
    return jax.shard_map(
        shards,
        mesh=Mesh(mesh.devices.reshape(sizes), AXES),
        in_specs=(
            P(AXES, None),
            P(AXES),
            P(ROW, COL, None, None, None),
            P(ROW, COL, None),
            P(ROW, COL, None),
            P(ROW, COL),
        ),
        out_specs=(P(AXES, None), P()),
        check_vma=False,
    )
```

```python
import functools

import jax
import jax.numpy as jnp
from jax import lax
from jax.experimental import pallas as pl
from jax.experimental.pallas import tpu as pltpu
from jax.sharding import Mesh, PartitionSpec as P

HIGHEST = lax.Precision.HIGHEST
AXES = ("x", "z", "y", "core")
ROW = ("x", "z")
COL = ("y", "core")
CONTRACT_LAST = (((1,), (1,)), ((), ()))


def exchange(chunks, axes):
    return lax.all_to_all(chunks, axes, 0, 0, tiled=True)


def to_all(value, axes):
    copies = lax.axis_size(axes)
    return exchange(jnp.broadcast_to(value[None], (copies, *value.shape)), axes)


def split(value):
    high = value.astype(jnp.bfloat16)
    return high, (value - high.astype(jnp.float32)).astype(jnp.bfloat16)


def dot_pieces(left, right):
    return lax.dot_general(left, right, CONTRACT_LAST, preferred_element_type=jnp.float32)


def add_slots(rows_ref, cols_ref, count_ref, blocks_ref, gathered_ref, sums_ref):
    sums_ref[...] = jnp.zeros_like(sums_ref)
    count = count_ref[0]
    width, nodes = sums_ref.shape[1:]
    pieces = gathered_ref.shape[1] // width
    for slot in range(blocks_ref.shape[0]):
        live = (slot < count).astype(jnp.float32)
        col = cols_ref[slot]
        first_row = pl.multiple_of((col % pieces) * width, width)
        vectors = jnp.concatenate(split(gathered_ref[col // pieces, pl.ds(first_row, width)] * live), axis=0)
        products = dot_pieces(vectors, jnp.concatenate(split(blocks_ref[slot]), axis=0))
        sums_ref[rows_ref[slot]] += products[:width, :nodes] + products[width:, :nodes] + products[:width, nodes:]


def tile_kernel(rows_ref, cols_ref, count_ref, blocks_ref, gathered_ref, out_ref):
    add_slots(rows_ref, cols_ref, count_ref, blocks_ref, gathered_ref, out_ref)


def tile_rider_kernel(rows_ref, cols_ref, count_ref, blocks_ref, gathered_ref, out_ref, rider_ref):
    add_slots(rows_ref, cols_ref, count_ref, blocks_ref, gathered_ref, out_ref)
    pieces_end = gathered_ref.shape[1] - rider_ref.shape[0]
    rider_ref[...] = jnp.sum(gathered_ref[:, pieces_end:], axis=0)


def project_kernel(
    rows_ref, cols_ref, count_ref, blocks_ref, gathered_ref, own_ref, gram_ref, out_ref, sums_ref
):
    add_slots(rows_ref, cols_ref, count_ref, blocks_ref, gathered_ref, sums_ref)
    row_blocks, width, _ = sums_ref.shape
    products = jnp.zeros((2 * width, 2 * width), jnp.float32)
    for piece in range(row_blocks):
        left = jnp.concatenate(split(own_ref[piece]), axis=0)
        right = jnp.concatenate(split(sums_ref[piece]), axis=0)
        products += dot_pieces(left, right)
    total = products[:width, :width] + products[:width, width:] + products[width:, :width] + products[width:, width:]
    out_ref[...] = jnp.concatenate([total, gram_ref[...]], axis=1)


def sum_kernel(chunks_ref, copies_ref):
    copies_ref[...] = jnp.broadcast_to(jnp.sum(chunks_ref[...], axis=0)[None], copies_ref.shape)


def inverse_factor(gram_matrix, pivots=4):
    size = gram_matrix.shape[0]
    shape = (size, 2 * size)
    row_of = lax.broadcasted_iota(jnp.int32, shape, 0)
    eye = (lax.broadcasted_iota(jnp.int32, (size, size), 0) == lax.broadcasted_iota(jnp.int32, (size, size), 1)).astype(
        jnp.float32
    )
    work = jnp.concatenate([gram_matrix, eye], axis=1)
    for first in range(0, size, pivots):
        columns = [jnp.broadcast_to(work[:, j : j + 1], shape) for j in range(first, first + pivots)]
        upper = [work[j : j + 1] for j in range(first, first + pivots)]
        taken = jnp.zeros(shape, jnp.float32)
        for k in range(pivots):
            inverse_pivot = 1.0 / columns[k][first + k : first + k + 1]
            upper[k] = upper[k] * inverse_pivot
            for m in range(k + 1, pivots):
                factor = columns[k][first + m : first + m + 1]
                upper[m] = upper[m] - factor * upper[k]
                columns[m] = columns[m] - columns[k] * (factor * inverse_pivot)
            taken += jnp.where(row_of > first + k, columns[k], 0.0) * upper[k]
        work = work - taken
    diagonal = jnp.sum(work[:, :size] * eye, axis=1, keepdims=True)
    return work[:, size:] * lax.rsqrt(diagonal)


def inverse_kernel(nodes_all, folded_ref, out_ref):
    out_ref[...] = inverse_factor(unfold(folded_ref[...]) / nodes_all)


def finish_kernel(nodes_all, both_ref, filtered_ref, basis_ref, ritz_ref):
    width = filtered_ref.shape[0]
    both = both_ref[...] / nodes_all
    inverse = inverse_factor(both[:, width:])
    half = jnp.dot(inverse, both[:, :width], precision=HIGHEST, preferred_element_type=jnp.float32)
    ritz_ref[...] = lax.dot_general(
        half, inverse, CONTRACT_LAST, precision=HIGHEST, preferred_element_type=jnp.float32
    )
    basis_ref[...] = jnp.dot(inverse, filtered_ref[...], precision=HIGHEST, preferred_element_type=jnp.float32)


SMEM = pl.BlockSpec(memory_space=pltpu.SMEM)
VMEM = pl.BlockSpec(memory_space=pltpu.VMEM)


def call_kernel(kernel, ins, outs, scratch=()):
    return pl.pallas_call(
        kernel,
        out_shape=[jax.ShapeDtypeStruct(shape, jnp.float32) for shape in outs],
        in_specs=[SMEM if value.dtype == jnp.int32 and value.ndim == 1 else VMEM for value in ins],
        out_specs=[VMEM] * len(outs),
        scratch_shapes=list(scratch),
        compiler_params=pltpu.CompilerParams(vmem_limit_bytes=24 * 2**20),
    )(*ins)


def gram(left, right):
    return lax.dot_general(left, right, CONTRACT_LAST, precision=HIGHEST)


def matmul(left, right):
    return jnp.dot(left, right, precision=HIGHEST)


def fold(square):
    half = square.shape[0] // 2
    return jnp.concatenate([square[:half], square[half:]], axis=1)


def unfold(folded):
    half = folded.shape[1] // 2
    return jnp.concatenate([folded[:, :half], folded[:, half:]], axis=0)


def shards(start, degrees, blocks, block_rows, block_cols, block_counts):
    row_devices = lax.axis_size(ROW)
    col_devices = lax.axis_size(COL)
    nodes, width = start.shape
    nodes_all = nodes * row_devices * col_devices
    tile_blocks = blocks.reshape(blocks.shape[2:])
    rows = block_rows.reshape(-1)
    cols = block_cols.reshape(-1)
    count = block_counts.reshape(-1)

    y_devices = lax.axis_size("y")
    tile = (rows, cols, count, tile_blocks)
    tile_core_first = ((rows % 2) * y_devices + rows // 2, cols, count, tile_blocks)
    sums_shape = (col_devices, width, nodes)

    def gather(value, axes):
        return lax.all_gather(value, axes, axis=0, tiled=False)

    def reduce_cols(partial):
        along_y = exchange(partial.reshape(y_devices, -1, nodes), "y").sum(0)
        return exchange(along_y.reshape(-1, width, nodes), "core").sum(0) * scale

    def reduce_core_first(partial):
        halves = exchange(partial.reshape(-1, y_devices * width, nodes), "core").sum(0)
        return exchange(halves.reshape(y_devices, width, nodes), "y").sum(0) * scale

    def together(*values):
        return lax.optimization_barrier(values)

    def sum_to(chunks, copies):
        return call_kernel(sum_kernel, (chunks,), [(copies, *chunks.shape[1:])])[0]

    first = start.T
    scale = jnp.sqrt(16.0 / degrees.astype(jnp.float32))[None, :]
    along_z = gather(first * scale, "z").reshape(-1, nodes)
    rider = gather(fold(gram(first, first)), COL).sum(0).reshape(lax.axis_size("core"), -1, nodes)
    half_shape = rider.shape[1:]
    rider = lax.dynamic_index_in_dim(rider, lax.axis_index("core"), keepdims=False)
    gathered, rider = together(to_all(along_z, "x"), rider)
    (partial,) = call_kernel(tile_kernel, (*tile_core_first, gathered), [sums_shape])
    once = reduce_core_first(partial)

    along_z = gather(jnp.concatenate([once * scale, rider], axis=0), "z")
    along_z = jnp.concatenate([along_z[:, :width].reshape(-1, nodes), along_z[:, width:].sum(0)], axis=0)
    partial, rider = call_kernel(tile_rider_kernel, (*tile, to_all(along_z, "x")), [sums_shape, half_shape])
    rider = gather(rider, "core").reshape(-1, nodes)
    (inverse,) = call_kernel(functools.partial(inverse_kernel, nodes_all), (rider,), [(width, width)])
    filtered = matmul(inverse, 2.0 * reduce_cols(partial) - first)

    scaled = filtered * scale
    gathered, own_rows = together(to_all(gather(scaled, "z").reshape(-1, nodes), "x"), gather(scaled, COL))
    (projected,) = call_kernel(
        project_kernel,
        (*tile, gathered, own_rows, gram(filtered, filtered)),
        [(width, 2 * width)],
        [pltpu.VMEM(sums_shape, jnp.float32)],
    )
    projected = exchange(projected.reshape(col_devices, -1, 2 * width), COL)
    projected = exchange(sum_to(projected, row_devices), ROW)
    projected = exchange(sum_to(projected, col_devices), COL).reshape(width, 2 * width)
    basis, ritz = call_kernel(
        functools.partial(finish_kernel, nodes_all), (projected, filtered), [(width, nodes), (width, width)]
    )
    return (basis.T, ritz)


def solution(mesh):
    sizes = (4, 16, 8, 2)
    return jax.shard_map(
        shards,
        mesh=Mesh(mesh.devices.reshape(sizes), AXES),
        in_specs=(
            P(AXES, None),
            P(AXES),
            P(ROW, COL, None, None, None),
            P(ROW, COL, None),
            P(ROW, COL, None),
            P(ROW, COL),
        ),
        out_specs=(P(AXES, None), P()),
        check_vma=False,
    )
```

```python
import functools

import jax
import jax.numpy as jnp
from jax import lax
from jax.experimental import pallas as pl
from jax.experimental.pallas import tpu as pltpu
from jax.sharding import Mesh, PartitionSpec as P

HIGHEST = lax.Precision.HIGHEST
AXES = ("x", "z", "y", "core")
ROW = ("x", "z")
COL = ("y", "core")
CONTRACT_LAST = (((1,), (1,)), ((), ()))


def exchange(chunks, axes):
    return lax.all_to_all(chunks, axes, 0, 0, tiled=True)


def to_all(value, axes):
    copies = lax.axis_size(axes)
    return exchange(jnp.broadcast_to(value[None], (copies, *value.shape)), axes)


def split(value):
    high = value.astype(jnp.bfloat16)
    return high, (value - high.astype(jnp.float32)).astype(jnp.bfloat16)


def dot_pieces(left, right):
    return lax.dot_general(left, right, CONTRACT_LAST, preferred_element_type=jnp.float32)


def add_slots(rows_ref, cols_ref, count_ref, blocks_ref, gathered_ref, sums_ref):
    sums_ref[...] = jnp.zeros_like(sums_ref)
    count = count_ref[0]
    width, nodes = sums_ref.shape[1:]
    pieces = gathered_ref.shape[1] // width
    for slot in range(blocks_ref.shape[0]):
        live = (slot < count).astype(jnp.float32)
        col = cols_ref[slot]
        first_row = pl.multiple_of((col % pieces) * width, width)
        vectors = jnp.concatenate(split(gathered_ref[col // pieces, pl.ds(first_row, width)] * live), axis=0)
        products = dot_pieces(vectors, jnp.concatenate(split(blocks_ref[slot]), axis=0))
        sums_ref[rows_ref[slot]] += products[:width, :nodes] + products[width:, :nodes] + products[:width, nodes:]


def tile_kernel(rows_ref, cols_ref, count_ref, blocks_ref, gathered_ref, out_ref):
    add_slots(rows_ref, cols_ref, count_ref, blocks_ref, gathered_ref, out_ref)


def tile_rider_kernel(rows_ref, cols_ref, count_ref, blocks_ref, gathered_ref, out_ref, rider_ref):
    add_slots(rows_ref, cols_ref, count_ref, blocks_ref, gathered_ref, out_ref)
    pieces_end = gathered_ref.shape[1] - rider_ref.shape[0]
    rider_ref[...] = jnp.sum(gathered_ref[:, pieces_end:], axis=0)


def project_kernel(
    rows_ref, cols_ref, count_ref, blocks_ref, gathered_ref, own_ref, gram_ref, out_ref, sums_ref
):
    add_slots(rows_ref, cols_ref, count_ref, blocks_ref, gathered_ref, sums_ref)
    row_blocks, width, _ = sums_ref.shape
    products = jnp.zeros((2 * width, 2 * width), jnp.float32)
    for piece in range(row_blocks):
        left = jnp.concatenate(split(own_ref[piece]), axis=0)
        right = jnp.concatenate(split(sums_ref[piece]), axis=0)
        products += dot_pieces(left, right)
    total = products[:width, :width] + products[:width, width:] + products[width:, :width] + products[width:, width:]
    out_ref[...] = jnp.concatenate([total, gram_ref[...]], axis=1)


def sum_kernel(chunks_ref, copies_ref):
    copies_ref[...] = jnp.broadcast_to(jnp.sum(chunks_ref[...], axis=0)[None], copies_ref.shape)


def inverse_factor(gram_matrix, pivots=4):
    size = gram_matrix.shape[0]
    shape = (size, 2 * size)
    row_of = lax.broadcasted_iota(jnp.int32, shape, 0)
    eye = (lax.broadcasted_iota(jnp.int32, (size, size), 0) == lax.broadcasted_iota(jnp.int32, (size, size), 1)).astype(
        jnp.float32
    )
    work = jnp.concatenate([gram_matrix, eye], axis=1)
    for first in range(0, size, pivots):
        columns = [jnp.broadcast_to(work[:, j : j + 1], shape) for j in range(first, first + pivots)]
        upper = [work[j : j + 1] for j in range(first, first + pivots)]
        taken = jnp.zeros(shape, jnp.float32)
        for k in range(pivots):
            inverse_pivot = 1.0 / columns[k][first + k : first + k + 1]
            upper[k] = upper[k] * inverse_pivot
            for m in range(k + 1, pivots):
                factor = columns[k][first + m : first + m + 1]
                upper[m] = upper[m] - factor * upper[k]
                columns[m] = columns[m] - columns[k] * (factor * inverse_pivot)
            taken += jnp.where(row_of > first + k, columns[k], 0.0) * upper[k]
        work = work - taken
    diagonal = jnp.sum(work[:, :size] * eye, axis=1, keepdims=True)
    return work[:, size:] * lax.rsqrt(diagonal)


def inverse_kernel(nodes_all, folded_ref, out_ref):
    out_ref[...] = inverse_factor(unfold(folded_ref[...]) / nodes_all)


def finish_kernel(nodes_all, both_ref, filtered_ref, basis_ref, ritz_ref):
    width = filtered_ref.shape[0]
    both = both_ref[...] / nodes_all
    inverse = inverse_factor(both[:, width:])
    half = jnp.dot(inverse, both[:, :width], precision=HIGHEST, preferred_element_type=jnp.float32)
    ritz_ref[...] = lax.dot_general(
        half, inverse, CONTRACT_LAST, precision=HIGHEST, preferred_element_type=jnp.float32
    )
    basis_ref[...] = jnp.dot(inverse, filtered_ref[...], precision=HIGHEST, preferred_element_type=jnp.float32)


SMEM = pl.BlockSpec(memory_space=pltpu.SMEM)
VMEM = pl.BlockSpec(memory_space=pltpu.VMEM)


def call_kernel(kernel, ins, outs, scratch=()):
    return pl.pallas_call(
        kernel,
        out_shape=[jax.ShapeDtypeStruct(shape, jnp.float32) for shape in outs],
        in_specs=[SMEM if value.dtype == jnp.int32 and value.ndim == 1 else VMEM for value in ins],
        out_specs=[VMEM] * len(outs),
        scratch_shapes=list(scratch),
        compiler_params=pltpu.CompilerParams(vmem_limit_bytes=24 * 2**20),
    )(*ins)


def gram(left, right):
    return lax.dot_general(left, right, CONTRACT_LAST, precision=HIGHEST)


def matmul(left, right):
    return jnp.dot(left, right, precision=HIGHEST)


def fold(square):
    half = square.shape[0] // 2
    return jnp.concatenate([square[:half], square[half:]], axis=1)


def unfold(folded):
    half = folded.shape[1] // 2
    return jnp.concatenate([folded[:, :half], folded[:, half:]], axis=0)


def shards(start, degrees, blocks, block_rows, block_cols, block_counts):
    row_devices = lax.axis_size(ROW)
    col_devices = lax.axis_size(COL)
    nodes, width = start.shape
    nodes_all = nodes * row_devices * col_devices
    tile_blocks = blocks.reshape(blocks.shape[2:])
    rows = block_rows.reshape(-1)
    cols = block_cols.reshape(-1)
    count = block_counts.reshape(-1)

    y_devices = lax.axis_size("y")
    tile = (rows, cols, count, tile_blocks)
    tile_core_first = ((rows % 2) * y_devices + rows // 2, cols, count, tile_blocks)
    sums_shape = (col_devices, width, nodes)

    def gather(value, axes):
        return lax.all_gather(value, axes, axis=0, tiled=False)

    def reduce_cols(partial):
        halves = exchange(partial.reshape(-1, y_devices * width, nodes), "core").sum(0)
        return exchange(halves.reshape(y_devices, width, nodes), "y").sum(0) * scale

    def together(*values):
        return lax.optimization_barrier(values)

    def sum_to(chunks, copies):
        return call_kernel(sum_kernel, (chunks,), [(copies, *chunks.shape[1:])])[0]

    first = start.T
    scale = jnp.sqrt(16.0 / degrees.astype(jnp.float32))[None, :]
    along_z = gather(first * scale, "z").reshape(-1, nodes)
    rider = gather(fold(gram(first, first)), COL).sum(0).reshape(lax.axis_size("core"), -1, nodes)
    half_shape = rider.shape[1:]
    rider = lax.dynamic_index_in_dim(rider, lax.axis_index("core"), keepdims=False)
    gathered, rider = together(to_all(along_z, "x"), rider)
    (partial,) = call_kernel(tile_kernel, (*tile_core_first, gathered), [sums_shape])
    once = reduce_cols(partial)

    along_z = gather(jnp.concatenate([once * scale, rider], axis=0), "z")
    along_z = jnp.concatenate([along_z[:, :width].reshape(-1, nodes), along_z[:, width:].sum(0)], axis=0)
    partial, rider = call_kernel(tile_rider_kernel, (*tile_core_first, to_all(along_z, "x")), [sums_shape, half_shape])
    rider = gather(rider, "core").reshape(-1, nodes)
    (inverse,) = call_kernel(functools.partial(inverse_kernel, nodes_all), (rider,), [(width, width)])
    filtered = matmul(inverse, 2.0 * reduce_cols(partial) - first)

    scaled = filtered * scale
    gathered, own_rows = together(to_all(gather(scaled, "z").reshape(-1, nodes), "x"), gather(scaled, COL))
    (projected,) = call_kernel(
        project_kernel,
        (*tile, gathered, own_rows, gram(filtered, filtered)),
        [(width, 2 * width)],
        [pltpu.VMEM(sums_shape, jnp.float32)],
    )
    projected = exchange(projected.reshape(col_devices, -1, 2 * width), COL)
    projected = exchange(sum_to(projected, row_devices), ROW)
    projected = exchange(sum_to(projected, col_devices), COL).reshape(width, 2 * width)
    basis, ritz = call_kernel(
        functools.partial(finish_kernel, nodes_all), (projected, filtered), [(width, nodes), (width, width)]
    )
    return (basis.T, ritz)


def solution(mesh):
    sizes = (4, 16, 8, 2)
    return jax.shard_map(
        shards,
        mesh=Mesh(mesh.devices.reshape(sizes), AXES),
        in_specs=(
            P(AXES, None),
            P(AXES),
            P(ROW, COL, None, None, None),
            P(ROW, COL, None),
            P(ROW, COL, None),
            P(ROW, COL),
        ),
        out_specs=(P(AXES, None), P()),
        check_vma=False,
    )
```

```python
import functools

import jax
import jax.numpy as jnp
from jax import lax
from jax.experimental import pallas as pl
from jax.experimental.pallas import tpu as pltpu
from jax.sharding import Mesh, PartitionSpec as P

HIGHEST = lax.Precision.HIGHEST
AXES = ("x", "z", "y", "core")
ROW = ("x", "z")
COL = ("y", "core")
CONTRACT_LAST = (((1,), (1,)), ((), ()))


def exchange(chunks, axes):
    return lax.all_to_all(chunks, axes, 0, 0, tiled=True)


def to_all(value, axes):
    copies = lax.axis_size(axes)
    return exchange(jnp.broadcast_to(value[None], (copies, *value.shape)), axes)


def split(value):
    high = value.astype(jnp.bfloat16)
    return high, (value - high.astype(jnp.float32)).astype(jnp.bfloat16)


def dot_pieces(left, right):
    return lax.dot_general(left, right, CONTRACT_LAST, preferred_element_type=jnp.float32)


def add_slots(rows_ref, cols_ref, count_ref, blocks_ref, gathered_ref, sums_ref, core_first=False):
    sums_ref[...] = jnp.zeros_like(sums_ref)
    half = sums_ref.shape[0] // 2
    width, nodes = sums_ref.shape[1:]
    count = jnp.broadcast_to(count_ref[...], (width, nodes))
    pieces = gathered_ref.shape[1] // width
    for slot in range(blocks_ref.shape[0]):
        row = rows_ref[slot]
        if core_first:
            row = (row % 2) * half + row // 2
        col = cols_ref[slot]
        first_row = pl.multiple_of((col % pieces) * width, width)
        piece = jnp.where(slot < count, gathered_ref[col // pieces, pl.ds(first_row, width)], 0.0)
        vectors = jnp.concatenate(split(piece), axis=0)
        products = dot_pieces(vectors, jnp.concatenate(split(blocks_ref[slot]), axis=0))
        sums_ref[row] += products[:width, :nodes] + products[width:, :nodes] + products[:width, nodes:]


def tile_kernel(rows_ref, cols_ref, count_ref, blocks_ref, gathered_ref, out_ref):
    add_slots(rows_ref, cols_ref, count_ref, blocks_ref, gathered_ref, out_ref, core_first=True)


def tile_rider_kernel(rows_ref, cols_ref, count_ref, blocks_ref, gathered_ref, out_ref, rider_ref):
    add_slots(rows_ref, cols_ref, count_ref, blocks_ref, gathered_ref, out_ref, core_first=True)
    pieces_end = gathered_ref.shape[1] - rider_ref.shape[0]
    rider_ref[...] = jnp.sum(gathered_ref[:, pieces_end:], axis=0)


def project_kernel(
    rows_ref, cols_ref, count_ref, blocks_ref, gathered_ref, own_ref, gram_ref, out_ref, sums_ref
):
    add_slots(rows_ref, cols_ref, count_ref, blocks_ref, gathered_ref, sums_ref)
    row_blocks, width, _ = sums_ref.shape
    products = jnp.zeros((2 * width, 2 * width), jnp.float32)
    for piece in range(row_blocks):
        left = jnp.concatenate(split(own_ref[piece]), axis=0)
        right = jnp.concatenate(split(sums_ref[piece]), axis=0)
        products += dot_pieces(left, right)
    total = products[:width, :width] + products[:width, width:] + products[width:, :width] + products[width:, width:]
    out_ref[...] = jnp.concatenate([total, gram_ref[...]], axis=1)


def sum_kernel(chunks_ref, copies_ref):
    copies_ref[...] = jnp.broadcast_to(jnp.sum(chunks_ref[...], axis=0)[None], copies_ref.shape)


def inverse_factor(gram_matrix, pivots=4):
    size = gram_matrix.shape[0]
    shape = (size, 2 * size)
    row_of = lax.broadcasted_iota(jnp.int32, shape, 0)
    eye = (lax.broadcasted_iota(jnp.int32, (size, size), 0) == lax.broadcasted_iota(jnp.int32, (size, size), 1)).astype(
        jnp.float32
    )
    work = jnp.concatenate([gram_matrix, eye], axis=1)
    for first in range(0, size, pivots):
        columns = [jnp.broadcast_to(work[:, j : j + 1], shape) for j in range(first, first + pivots)]
        upper = [work[j : j + 1] for j in range(first, first + pivots)]
        taken = jnp.zeros(shape, jnp.float32)
        for k in range(pivots):
            inverse_pivot = 1.0 / columns[k][first + k : first + k + 1]
            upper[k] = upper[k] * inverse_pivot
            for m in range(k + 1, pivots):
                factor = columns[k][first + m : first + m + 1]
                upper[m] = upper[m] - factor * upper[k]
                columns[m] = columns[m] - columns[k] * (factor * inverse_pivot)
            taken += jnp.where(row_of > first + k, columns[k], 0.0) * upper[k]
        work = work - taken
    diagonal = jnp.sum(work[:, :size] * eye, axis=1, keepdims=True)
    return work[:, size:] * lax.rsqrt(diagonal)


def inverse_kernel(nodes_all, folded_ref, out_ref):
    out_ref[...] = inverse_factor(unfold(folded_ref[...]) / nodes_all)


def finish_kernel(nodes_all, both_ref, filtered_ref, basis_ref, ritz_ref):
    width = filtered_ref.shape[0]
    both = both_ref[...] / nodes_all
    inverse = inverse_factor(both[:, width:])
    half = jnp.dot(inverse, both[:, :width], precision=HIGHEST, preferred_element_type=jnp.float32)
    ritz_ref[...] = lax.dot_general(
        half, inverse, CONTRACT_LAST, precision=HIGHEST, preferred_element_type=jnp.float32
    )
    basis_ref[...] = jnp.dot(inverse, filtered_ref[...], precision=HIGHEST, preferred_element_type=jnp.float32)


SMEM = pl.BlockSpec(memory_space=pltpu.SMEM)
VMEM = pl.BlockSpec(memory_space=pltpu.VMEM)


def call_kernel(kernel, ins, outs, scratch=()):
    return pl.pallas_call(
        kernel,
        out_shape=[jax.ShapeDtypeStruct(shape, jnp.float32) for shape in outs],
        in_specs=[SMEM if value.ndim == 1 else VMEM for value in ins],
        out_specs=[VMEM] * len(outs),
        scratch_shapes=list(scratch),
        compiler_params=pltpu.CompilerParams(vmem_limit_bytes=24 * 2**20),
    )(*ins)


def gram(left, right):
    return lax.dot_general(left, right, CONTRACT_LAST, precision=HIGHEST)


def matmul(left, right):
    return jnp.dot(left, right, precision=HIGHEST)


def fold(square):
    half = square.shape[0] // 2
    return jnp.concatenate([square[:half], square[half:]], axis=1)


def unfold(folded):
    half = folded.shape[1] // 2
    return jnp.concatenate([folded[:, :half], folded[:, half:]], axis=0)


def shards(start, degrees, blocks, block_rows, block_cols, block_counts):
    row_devices = lax.axis_size(ROW)
    col_devices = lax.axis_size(COL)
    nodes, width = start.shape
    nodes_all = nodes * row_devices * col_devices
    tile_blocks = blocks.reshape(blocks.shape[2:])
    rows = block_rows.reshape(-1)
    cols = block_cols.reshape(-1)
    tile = (rows, cols, block_counts, tile_blocks)
    y_devices = lax.axis_size("y")
    sums_shape = (col_devices, width, nodes)

    def gather(value, axes):
        return lax.all_gather(value, axes, axis=0, tiled=False)

    def reduce_cols(partial, rider=None):
        halves = partial.reshape(-1, y_devices * width, nodes)
        if rider is not None:
            halves = jnp.concatenate([halves, rider], axis=1)
        halves = exchange(halves, "core").sum(0)
        cut = y_devices * width
        chunks = halves[:cut].reshape(y_devices, width, nodes)
        if rider is None:
            return exchange(chunks, "y").sum(0) * scale
        rest = jnp.broadcast_to(halves[cut:][None], (y_devices, *rider.shape[1:]))
        done = exchange(jnp.concatenate([chunks, rest], axis=1), "y").sum(0)
        return done[:width] * scale, done[width:]

    def together(*values):
        return lax.optimization_barrier(values)

    def sum_to(chunks, copies):
        return call_kernel(sum_kernel, (chunks,), [(copies, *chunks.shape[1:])])[0]

    first = start.T
    scale = jnp.sqrt(16.0 / degrees.astype(jnp.float32))[None, :]
    along_z = gather(first * scale, "z").reshape(-1, nodes)
    gathered, ordered = together(to_all(along_z, "x"), first)
    (partial,) = call_kernel(tile_kernel, (*tile, gathered), [sums_shape])
    rider = fold(gram(ordered, ordered)).reshape(lax.axis_size("core"), -1, nodes)
    half_shape = rider.shape[1:]
    once, rider = reduce_cols(partial, rider)

    along_z = gather(jnp.concatenate([once * scale, rider], axis=0), "z")
    along_z = jnp.concatenate([along_z[:, :width].reshape(-1, nodes), along_z[:, width:].sum(0)], axis=0)
    partial, rider = call_kernel(tile_rider_kernel, (*tile, to_all(along_z, "x")), [sums_shape, half_shape])
    rider = gather(rider, "core").reshape(-1, nodes)
    (inverse,) = call_kernel(functools.partial(inverse_kernel, nodes_all), (rider,), [(width, width)])
    filtered = matmul(inverse, 2.0 * reduce_cols(partial) - first)

    scaled = filtered * scale
    gathered, own_rows = together(to_all(gather(scaled, "z").reshape(-1, nodes), "x"), gather(scaled, COL))
    (projected,) = call_kernel(
        project_kernel,
        (*tile, gathered, own_rows, gram(filtered, filtered)),
        [(width, 2 * width)],
        [pltpu.VMEM(sums_shape, jnp.float32)],
    )
    projected = exchange(projected.reshape(col_devices, -1, 2 * width), COL)
    projected = exchange(sum_to(projected, row_devices), ROW)
    projected = exchange(sum_to(projected, col_devices), COL).reshape(width, 2 * width)
    basis, ritz = call_kernel(
        functools.partial(finish_kernel, nodes_all), (projected, filtered), [(width, nodes), (width, width)]
    )
    return (basis.T, ritz)


def solution(mesh):
    sizes = (4, 16, 8, 2)
    return jax.shard_map(
        shards,
        mesh=Mesh(mesh.devices.reshape(sizes), AXES),
        in_specs=(
            P(AXES, None),
            P(AXES),
            P(ROW, COL, None, None, None),
            P(ROW, COL, None),
            P(ROW, COL, None),
            P(ROW, COL),
        ),
        out_specs=(P(AXES, None), P()),
        check_vma=False,
    )
```

```python
import functools

import jax
import jax.numpy as jnp
from jax import lax
from jax.experimental import pallas as pl
from jax.experimental.pallas import tpu as pltpu
from jax.sharding import Mesh, PartitionSpec as P

HIGHEST = lax.Precision.HIGHEST
AXES = ("x", "z", "y", "core")
ROW = ("x", "z")
COL = ("y", "core")
CONTRACT_LAST = (((1,), (1,)), ((), ()))


def exchange(chunks, axes):
    return lax.all_to_all(chunks, axes, 0, 0, tiled=True)


def to_all(value, axes):
    copies = lax.axis_size(axes)
    return exchange(jnp.broadcast_to(value[None], (copies, *value.shape)), axes)


def split(value):
    high = value.astype(jnp.bfloat16)
    return high, (value - high.astype(jnp.float32)).astype(jnp.bfloat16)


def dot_pieces(left, right):
    return lax.dot_general(left, right, CONTRACT_LAST, preferred_element_type=jnp.float32)


def add_slots(rows_ref, cols_ref, count_ref, blocks_ref, gathered_ref, sums_ref):
    sums_ref[...] = jnp.zeros_like(sums_ref)
    count = count_ref[0]
    width, nodes = sums_ref.shape[1:]
    pieces = gathered_ref.shape[1] // width
    for slot in range(blocks_ref.shape[0]):
        live = (slot < count).astype(jnp.float32)
        col = cols_ref[slot]
        first_row = pl.multiple_of((col % pieces) * width, width)
        vectors = jnp.concatenate(split(gathered_ref[col // pieces, pl.ds(first_row, width)] * live), axis=0)
        products = dot_pieces(vectors, jnp.concatenate(split(blocks_ref[slot]), axis=0))
        sums_ref[rows_ref[slot]] += products[:width, :nodes] + products[width:, :nodes] + products[:width, nodes:]


def tile_kernel(rows_ref, cols_ref, count_ref, blocks_ref, gathered_ref, out_ref):
    add_slots(rows_ref, cols_ref, count_ref, blocks_ref, gathered_ref, out_ref)


def tile_rider_kernel(rows_ref, cols_ref, count_ref, blocks_ref, gathered_ref, out_ref, rider_ref):
    add_slots(rows_ref, cols_ref, count_ref, blocks_ref, gathered_ref, out_ref)
    pieces_end = gathered_ref.shape[1] - rider_ref.shape[0]
    rider_ref[...] = jnp.sum(gathered_ref[:, pieces_end:], axis=0)


def project_kernel(
    rows_ref, cols_ref, count_ref, blocks_ref, gathered_ref, own_ref, gram_ref, out_ref, sums_ref
):
    add_slots(rows_ref, cols_ref, count_ref, blocks_ref, gathered_ref, sums_ref)
    row_blocks, width, _ = sums_ref.shape
    products = jnp.zeros((2 * width, 2 * width), jnp.float32)
    for piece in range(row_blocks):
        left = jnp.concatenate(split(own_ref[piece]), axis=0)
        right = jnp.concatenate(split(sums_ref[piece]), axis=0)
        products += dot_pieces(left, right)
    total = products[:width, :width] + products[:width, width:] + products[width:, :width] + products[width:, width:]
    out_ref[...] = jnp.concatenate([total, gram_ref[...]], axis=1)


def sum_kernel(chunks_ref, copies_ref):
    copies_ref[...] = jnp.broadcast_to(jnp.sum(chunks_ref[...], axis=0)[None], copies_ref.shape)


def inverse_factor(gram_matrix, pivots=4):
    size = gram_matrix.shape[0]
    shape = (size, 2 * size)
    row_of = lax.broadcasted_iota(jnp.int32, shape, 0)
    eye = (lax.broadcasted_iota(jnp.int32, (size, size), 0) == lax.broadcasted_iota(jnp.int32, (size, size), 1)).astype(
        jnp.float32
    )
    work = jnp.concatenate([gram_matrix, eye], axis=1)
    for first in range(0, size, pivots):
        columns = [jnp.broadcast_to(work[:, j : j + 1], shape) for j in range(first, first + pivots)]
        upper = [work[j : j + 1] for j in range(first, first + pivots)]
        taken = jnp.zeros(shape, jnp.float32)
        for k in range(pivots):
            inverse_pivot = 1.0 / columns[k][first + k : first + k + 1]
            upper[k] = upper[k] * inverse_pivot
            for m in range(k + 1, pivots):
                factor = columns[k][first + m : first + m + 1]
                upper[m] = upper[m] - factor * upper[k]
                columns[m] = columns[m] - columns[k] * (factor * inverse_pivot)
            taken += jnp.where(row_of > first + k, columns[k], 0.0) * upper[k]
        work = work - taken
    diagonal = jnp.sum(work[:, :size] * eye, axis=1, keepdims=True)
    return work[:, size:] * lax.rsqrt(diagonal)


def inverse_kernel(nodes_all, folded_ref, out_ref):
    out_ref[...] = inverse_factor(unfold(folded_ref[...]) / nodes_all)


def finish_kernel(nodes_all, both_ref, filtered_ref, basis_ref, ritz_ref):
    width = filtered_ref.shape[0]
    both = jnp.sum(both_ref[...], axis=0) / nodes_all
    inverse = inverse_factor(both[:, width:])
    half = jnp.dot(inverse, both[:, :width], precision=HIGHEST, preferred_element_type=jnp.float32)
    ritz_ref[...] = lax.dot_general(
        half, inverse, CONTRACT_LAST, precision=HIGHEST, preferred_element_type=jnp.float32
    )
    basis_ref[...] = jnp.dot(inverse, filtered_ref[...], precision=HIGHEST, preferred_element_type=jnp.float32)


SMEM = pl.BlockSpec(memory_space=pltpu.SMEM)
VMEM = pl.BlockSpec(memory_space=pltpu.VMEM)


def call_kernel(kernel, ins, outs, scratch=()):
    return pl.pallas_call(
        kernel,
        out_shape=[jax.ShapeDtypeStruct(shape, jnp.float32) for shape in outs],
        in_specs=[SMEM if value.dtype == jnp.int32 and value.ndim == 1 else VMEM for value in ins],
        out_specs=[VMEM] * len(outs),
        scratch_shapes=list(scratch),
        compiler_params=pltpu.CompilerParams(vmem_limit_bytes=24 * 2**20),
    )(*ins)


def gram(left, right):
    return lax.dot_general(left, right, CONTRACT_LAST, precision=HIGHEST)


def matmul(left, right):
    return jnp.dot(left, right, precision=HIGHEST)


def fold(square):
    half = square.shape[0] // 2
    return jnp.concatenate([square[:half], square[half:]], axis=1)


def unfold(folded):
    half = folded.shape[1] // 2
    return jnp.concatenate([folded[:, :half], folded[:, half:]], axis=0)


def shards(start, degrees, blocks, block_rows, block_cols, block_counts):
    row_devices = lax.axis_size(ROW)
    col_devices = lax.axis_size(COL)
    nodes, width = start.shape
    nodes_all = nodes * row_devices * col_devices
    tile_blocks = blocks.reshape(blocks.shape[2:])
    rows = block_rows.reshape(-1)
    cols = block_cols.reshape(-1)
    count = block_counts.reshape(-1)

    y_devices = lax.axis_size("y")
    tile = (rows, cols, count, tile_blocks)
    tile_core_first = ((rows % 2) * y_devices + rows // 2, cols, count, tile_blocks)
    sums_shape = (col_devices, width, nodes)

    def gather(value, axes):
        return lax.all_gather(value, axes, axis=0, tiled=False)

    def reduce_cols(partial):
        halves = exchange(partial.reshape(-1, y_devices * width, nodes), "core").sum(0)
        return exchange(halves.reshape(y_devices, width, nodes), "y").sum(0) * scale

    def together(*values):
        return lax.optimization_barrier(values)

    def sum_to(chunks, copies):
        return call_kernel(sum_kernel, (chunks,), [(copies, *chunks.shape[1:])])[0]

    first = start.T
    scale = jnp.sqrt(16.0 / degrees.astype(jnp.float32))[None, :]
    along_z = gather(first * scale, "z").reshape(-1, nodes)
    rider = gather(fold(gram(first, first)), COL).sum(0).reshape(lax.axis_size("core"), -1, nodes)
    half_shape = rider.shape[1:]
    rider = lax.dynamic_index_in_dim(rider, lax.axis_index("core"), keepdims=False)
    gathered, rider = together(to_all(along_z, "x"), rider)
    (partial,) = call_kernel(tile_kernel, (*tile_core_first, gathered), [sums_shape])
    once = reduce_cols(partial)

    along_z = gather(jnp.concatenate([once * scale, rider], axis=0), "z")
    along_z = jnp.concatenate([along_z[:, :width].reshape(-1, nodes), along_z[:, width:].sum(0)], axis=0)
    partial, rider = call_kernel(tile_rider_kernel, (*tile_core_first, to_all(along_z, "x")), [sums_shape, half_shape])
    rider = gather(rider, "core").reshape(-1, nodes)
    (inverse,) = call_kernel(functools.partial(inverse_kernel, nodes_all), (rider,), [(width, width)])
    filtered = matmul(inverse, 2.0 * reduce_cols(partial) - first)

    scaled = filtered * scale
    gathered, own_rows = together(to_all(gather(scaled, "z").reshape(-1, nodes), "x"), gather(scaled, COL))
    (projected,) = call_kernel(
        project_kernel,
        (*tile, gathered, own_rows, gram(filtered, filtered)),
        [(width, 2 * width)],
        [pltpu.VMEM(sums_shape, jnp.float32)],
    )
    projected = exchange(projected.reshape(col_devices, -1, 2 * width), COL)
    projected = exchange(sum_to(projected, lax.axis_size("z")), "z")
    everywhere = ("x", "y", "core")
    projected = exchange(sum_to(projected, lax.axis_size(everywhere)), everywhere)
    projected = projected.reshape(lax.axis_size("x"), width, 2 * width)
    basis, ritz = call_kernel(
        functools.partial(finish_kernel, nodes_all), (projected, filtered), [(width, nodes), (width, width)]
    )
    return (basis.T, ritz)


def solution(mesh):
    sizes = (4, 16, 8, 2)
    return jax.shard_map(
        shards,
        mesh=Mesh(mesh.devices.reshape(sizes), AXES),
        in_specs=(
            P(AXES, None),
            P(AXES),
            P(ROW, COL, None, None, None),
            P(ROW, COL, None),
            P(ROW, COL, None),
            P(ROW, COL),
        ),
        out_specs=(P(AXES, None), P()),
        check_vma=False,
    )
```

```python
import functools

import jax
import jax.numpy as jnp
from jax import lax
from jax.experimental import pallas as pl
from jax.experimental.pallas import tpu as pltpu
from jax.sharding import Mesh, PartitionSpec as P

HIGHEST = lax.Precision.HIGHEST
AXES = ("x", "z", "y", "core")
ROW = ("x", "z")
COL = ("y", "core")
CONTRACT_LAST = (((1,), (1,)), ((), ()))


def exchange(chunks, axes):
    return lax.all_to_all(chunks, axes, 0, 0, tiled=True)


def to_all(value, axes):
    copies = lax.axis_size(axes)
    return exchange(jnp.broadcast_to(value[None], (copies, *value.shape)), axes)


def split(value):
    high = value.astype(jnp.bfloat16)
    return high, (value - high.astype(jnp.float32)).astype(jnp.bfloat16)


def dot_pieces(left, right):
    return lax.dot_general(left, right, CONTRACT_LAST, preferred_element_type=jnp.float32)


def add_slots(rows_ref, cols_ref, count_ref, blocks_ref, gathered_ref, sums_ref):
    sums_ref[...] = jnp.zeros_like(sums_ref)
    count = count_ref[0]
    width, nodes = sums_ref.shape[1:]
    pieces = gathered_ref.shape[1] // width
    for slot in range(blocks_ref.shape[0]):
        live = (slot < count).astype(jnp.float32)
        col = cols_ref[slot]
        first_row = pl.multiple_of((col % pieces) * width, width)
        vectors = jnp.concatenate(split(gathered_ref[col // pieces, pl.ds(first_row, width)] * live), axis=0)
        products = dot_pieces(vectors, jnp.concatenate(split(blocks_ref[slot]), axis=0))
        sums_ref[rows_ref[slot]] += products[:width, :nodes] + products[width:, :nodes] + products[:width, nodes:]


def tile_kernel(rows_ref, cols_ref, count_ref, blocks_ref, gathered_ref, out_ref):
    add_slots(rows_ref, cols_ref, count_ref, blocks_ref, gathered_ref, out_ref)


def tile_rider_kernel(rows_ref, cols_ref, count_ref, blocks_ref, gathered_ref, out_ref, rider_ref):
    add_slots(rows_ref, cols_ref, count_ref, blocks_ref, gathered_ref, out_ref)
    pieces_end = gathered_ref.shape[1] - rider_ref.shape[0]
    rider_ref[...] = jnp.sum(gathered_ref[:, pieces_end:], axis=0)


def project_kernel(
    rows_ref, cols_ref, count_ref, blocks_ref, gathered_ref, own_ref, gram_ref, out_ref, sums_ref
):
    add_slots(rows_ref, cols_ref, count_ref, blocks_ref, gathered_ref, sums_ref)
    row_blocks, width, _ = sums_ref.shape
    products = jnp.zeros((2 * width, 2 * width), jnp.float32)
    for piece in range(row_blocks):
        left = jnp.concatenate(split(own_ref[piece]), axis=0)
        right = jnp.concatenate(split(sums_ref[piece]), axis=0)
        products += dot_pieces(left, right)
    total = products[:width, :width] + products[:width, width:] + products[width:, :width] + products[width:, width:]
    out_ref[...] = jnp.concatenate([total, gram_ref[...]], axis=1)


def sum_kernel(chunks_ref, copies_ref):
    copies_ref[...] = jnp.broadcast_to(jnp.sum(chunks_ref[...], axis=0)[None], copies_ref.shape)


def inverse_factor(gram_matrix, pivots=8):
    size = gram_matrix.shape[0]
    shape = (size, 2 * size)
    row_of = lax.broadcasted_iota(jnp.int32, shape, 0)
    eye = (lax.broadcasted_iota(jnp.int32, (size, size), 0) == lax.broadcasted_iota(jnp.int32, (size, size), 1)).astype(
        jnp.float32
    )
    work = jnp.concatenate([gram_matrix, eye], axis=1)
    for first in range(0, size, pivots):
        columns = [jnp.broadcast_to(work[:, j : j + 1], shape) for j in range(first, first + pivots)]
        upper = [work[j : j + 1] for j in range(first, first + pivots)]
        taken = jnp.zeros(shape, jnp.float32)
        for k in range(pivots):
            inverse_pivot = 1.0 / columns[k][first + k : first + k + 1]
            upper[k] = upper[k] * inverse_pivot
            for m in range(k + 1, pivots):
                factor = columns[k][first + m : first + m + 1]
                upper[m] = upper[m] - factor * upper[k]
                columns[m] = columns[m] - columns[k] * (factor * inverse_pivot)
            taken += jnp.where(row_of > first + k, columns[k], 0.0) * upper[k]
        work = work - taken
    diagonal = jnp.sum(work[:, :size] * eye, axis=1, keepdims=True)
    return work[:, size:] * lax.rsqrt(diagonal)


def inverse_kernel(nodes_all, folded_ref, out_ref):
    out_ref[...] = inverse_factor(unfold(folded_ref[...]) / nodes_all)


def finish_kernel(nodes_all, both_ref, filtered_ref, basis_ref, ritz_ref):
    width = filtered_ref.shape[0]
    both = jnp.sum(both_ref[...], axis=0) / nodes_all
    inverse = inverse_factor(both[:, width:])
    half = jnp.dot(inverse, both[:, :width], precision=HIGHEST, preferred_element_type=jnp.float32)
    ritz_ref[...] = lax.dot_general(
        half, inverse, CONTRACT_LAST, precision=HIGHEST, preferred_element_type=jnp.float32
    )
    basis_ref[...] = jnp.dot(inverse, filtered_ref[...], precision=HIGHEST, preferred_element_type=jnp.float32)


SMEM = pl.BlockSpec(memory_space=pltpu.SMEM)
VMEM = pl.BlockSpec(memory_space=pltpu.VMEM)


def call_kernel(kernel, ins, outs, scratch=()):
    return pl.pallas_call(
        kernel,
        out_shape=[jax.ShapeDtypeStruct(shape, jnp.float32) for shape in outs],
        in_specs=[SMEM if value.dtype == jnp.int32 and value.ndim == 1 else VMEM for value in ins],
        out_specs=[VMEM] * len(outs),
        scratch_shapes=list(scratch),
        compiler_params=pltpu.CompilerParams(vmem_limit_bytes=24 * 2**20),
    )(*ins)


def gram(left, right):
    return lax.dot_general(left, right, CONTRACT_LAST, precision=HIGHEST)


def matmul(left, right):
    return jnp.dot(left, right, precision=HIGHEST)


def fold(square):
    half = square.shape[0] // 2
    return jnp.concatenate([square[:half], square[half:]], axis=1)


def unfold(folded):
    half = folded.shape[1] // 2
    return jnp.concatenate([folded[:, :half], folded[:, half:]], axis=0)


def shards(start, degrees, blocks, block_rows, block_cols, block_counts):
    row_devices = lax.axis_size(ROW)
    col_devices = lax.axis_size(COL)
    nodes, width = start.shape
    nodes_all = nodes * row_devices * col_devices
    tile_blocks = blocks.reshape(blocks.shape[2:])
    rows = block_rows.reshape(-1)
    cols = block_cols.reshape(-1)
    count = block_counts.reshape(-1)

    y_devices = lax.axis_size("y")
    tile = (rows, cols, count, tile_blocks)
    tile_core_first = ((rows % 2) * y_devices + rows // 2, cols, count, tile_blocks)
    sums_shape = (col_devices, width, nodes)

    def gather(value, axes):
        return lax.all_gather(value, axes, axis=0, tiled=False)

    def reduce_cols(partial):
        halves = exchange(partial.reshape(-1, y_devices * width, nodes), "core").sum(0)
        return exchange(halves.reshape(y_devices, width, nodes), "y").sum(0) * scale

    def together(*values):
        return lax.optimization_barrier(values)

    def sum_to(chunks, copies):
        return call_kernel(sum_kernel, (chunks,), [(copies, *chunks.shape[1:])])[0]

    first = start.T
    scale = jnp.sqrt(16.0 / degrees.astype(jnp.float32))[None, :]
    along_z = gather(first * scale, "z").reshape(-1, nodes)
    rider = gather(fold(gram(first, first)), COL).sum(0).reshape(lax.axis_size("core"), -1, nodes)
    half_shape = rider.shape[1:]
    rider = lax.dynamic_index_in_dim(rider, lax.axis_index("core"), keepdims=False)
    gathered, rider = together(to_all(along_z, "x"), rider)
    (partial,) = call_kernel(tile_kernel, (*tile_core_first, gathered), [sums_shape])
    once = reduce_cols(partial)

    along_z = gather(jnp.concatenate([once * scale, rider], axis=0), "z")
    along_z = jnp.concatenate([along_z[:, :width].reshape(-1, nodes), along_z[:, width:].sum(0)], axis=0)
    partial, rider = call_kernel(tile_rider_kernel, (*tile_core_first, to_all(along_z, "x")), [sums_shape, half_shape])
    rider = gather(rider, "core").reshape(-1, nodes)
    (inverse,) = call_kernel(functools.partial(inverse_kernel, nodes_all), (rider,), [(width, width)])
    filtered = matmul(inverse, 2.0 * reduce_cols(partial) - first)

    scaled = filtered * scale
    gathered, own_rows = together(to_all(gather(scaled, "z").reshape(-1, nodes), "x"), gather(scaled, COL))
    (projected,) = call_kernel(
        project_kernel,
        (*tile, gathered, own_rows, gram(filtered, filtered)),
        [(width, 2 * width)],
        [pltpu.VMEM(sums_shape, jnp.float32)],
    )
    projected = exchange(projected.reshape(col_devices, -1, 2 * width), COL)
    projected = exchange(sum_to(projected, lax.axis_size("z")), "z")
    everywhere = ("x", "y", "core")
    projected = exchange(sum_to(projected, lax.axis_size(everywhere)), everywhere)
    projected = projected.reshape(lax.axis_size("x"), width, 2 * width)
    basis, ritz = call_kernel(
        functools.partial(finish_kernel, nodes_all), (projected, filtered), [(width, nodes), (width, width)]
    )
    return (basis.T, ritz)


def solution(mesh):
    sizes = (4, 16, 8, 2)
    return jax.shard_map(
        shards,
        mesh=Mesh(mesh.devices.reshape(sizes), AXES),
        in_specs=(
            P(AXES, None),
            P(AXES),
            P(ROW, COL, None, None, None),
            P(ROW, COL, None),
            P(ROW, COL, None),
            P(ROW, COL),
        ),
        out_specs=(P(AXES, None), P()),
        check_vma=False,
    )
```
